256 devices in a mesh: seq: 32 (over x, y, core), head: 8 (over z).
Axes of the slice: x: 4, y: 4, z: 8, core: 2. Of those that a mesh axis runs over, the one named last changes fastest.
Arguments:
- latent: bfloat16 [64, 4096], P('seq'), may hold values from -6 to 6
- pos_embed: bfloat16 [10752, 2048], P('seq', 'head'), may hold values from -3 to 3
- embed_weight: bfloat16 [32, 2048], P(None, 'head'), may hold values from -1 to 1
- norm_gain1: float32 [2048], replicated, may hold values from 0.1 to 1.9
- qkv_weight: bfloat16 [3, 2048, 2048], P(None, None, 'head'), may hold values from -1 to 1
- out_weight: bfloat16 [2048, 2048], P('head'), may hold values from -0.5 to 0.5
- norm_gain2: float32 [2048], replicated, may hold values from 0.1 to 1.9
- up_weight: bfloat16 [2048, 4096], P(None, 'head'), may hold values from -0.125 to 0.125
- down_weight: bfloat16 [4096, 2048], P('head'), may hold values from -0.09375 to 0.09375
Outputs:
- layer_out: bfloat16 [10752, 2048], P('seq', 'head')
The draws below stay inside these ranges and needn't reach their ends.
All inputs are finite; a program needn't handle non-finite values.
Results may differ from the reference program's by a relative error of at most 0.02.
Values may be sent and summed in bfloat16 or wider, within the bound.
A program may use at most 128 MiB of HBM per device.

```python
import jax
import jax.numpy as jnp
from jax import lax

D = 2048
HEADS = 16
HS = 128
FF = 4096
C = 32
W = 128
H = 64
N0 = 512
N1 = 2048
TOK_DEV = 336
TOKENS = 10752
N_SEQ = 32


def draw_qkv_weight(key, part):
    key = jax.random.fold_in(key, 7)
    first = jax.random.fold_in(key, 0)
    result = jax.random.normal(first, (3, D, D), jnp.float32) * D ** (-0.5)
    return jnp.clip(result, -1.0, 1.0).astype(jnp.bfloat16)


def level_of(rng, shape, shards, least, largest):
    loudness, own = 1.0, jax.random.fold_in(rng, 6)
    for dim, blocks in shards:
        steps = jnp.exp(jax.random.uniform(jax.random.fold_in(own, dim), (blocks,), jnp.float32, least / len(shards), largest / len(shards)))
        loudness = loudness * jnp.repeat(steps, shape[dim] // blocks).reshape([-1 if axis == dim else 1 for axis in range(len(shape))])
    return loudness


def gaussian(rng, extent, scale, limit, cuts=(), kind=jnp.bfloat16):
    values = jax.random.normal(rng, extent, jnp.float32) * scale
    if len(cuts) > 0:
        values = level_of(rng, extent, cuts, -0.22, 0.18) * values
    return jnp.clip(values, min=-limit, max=limit).astype(kind)


def setup_inputs(seed: int = 0) -> dict:
    streams_of = jax.random.split(jax.random.key(seed), 10)
    latent = gaussian(streams_of[0], (H, W * C), 1.0, 6.0, ((0, 32),))
    pos_embed = gaussian(streams_of[1], (TOKENS, D), 0.5, 3.0, ((0, 32), (1, 8)))
    embed_weight = gaussian(streams_of[2], (C, D), C ** -0.5, 1.0, ((1, 8),))
    norm_gain1 = jnp.clip(1.0 + 0.18 * jax.random.normal(streams_of[3], (D,), jnp.float32), 0.1, 1.9)
    qkv_weight = draw_qkv_weight(jax.random.fold_in(streams_of[9], 71), 0)
    out_weight = gaussian(streams_of[5], (D, D), (D // 16) ** -0.5, 0.5, ((0, 8),))
    norm_gain2 = jnp.clip(1.0 + 0.18 * jax.random.normal(streams_of[6], (D,), jnp.float32), 0.1, 1.9)
    up_weight = gaussian(streams_of[7], (D, FF), D ** -0.5, 0.125, ((1, 8),))
    down_weight = gaussian(streams_of[8], (FF, D), FF ** -0.5, 0.09375, ((0, 8),))
    return dict(latent=latent, pos_embed=pos_embed, embed_weight=embed_weight, norm_gain1=norm_gain1, qkv_weight=qkv_weight, out_weight=out_weight, norm_gain2=norm_gain2, up_weight=up_weight, down_weight=down_weight)


def rms_norm(values, gain):
    wide = values.astype(jnp.float32)
    scale = lax.rsqrt(lax.optimization_barrier(jnp.mean(wide * wide, axis=-1, keepdims=True)) + 1e-06)
    return (wide * scale * gain).astype(jnp.bfloat16)

def reference(latent, pos_embed, embed_weight, norm_gain1, qkv_weight, out_weight, norm_gain2, up_weight, down_weight):
    pixels = latent.astype(jnp.float32).reshape(H, W, C)
    pooled_mid = pixels.reshape(H // 2, 2, W // 2, 2, C).mean(axis=(1, 3))
    pooled_low = pixels.reshape(H // 4, 4, W // 4, 4, C).mean(axis=(1, 3))
    lifted_low = jnp.repeat(jnp.repeat(pooled_low, 2, axis=0), 2, axis=1)
    lifted_mid = jnp.repeat(jnp.repeat(pooled_mid, 2, axis=0), 2, axis=1)
    inputs = jnp.concatenate([pooled_low.reshape(-1, C), lifted_low.reshape(-1, C), lifted_mid.reshape(-1, C)], axis=0)
    stream = (jnp.dot(inputs, embed_weight.astype(jnp.float32), precision=lax.Precision.HIGHEST) + pos_embed.astype(jnp.float32)).astype(jnp.bfloat16)
    normed = rms_norm(stream, norm_gain1)
    projections = jnp.einsum('td,jde->jte', normed.astype(jnp.float32), qkv_weight.astype(jnp.float32)).astype(jnp.bfloat16)
    queries = projections[0].reshape(TOKENS, HEADS, HS).transpose(1, 0, 2)
    keys = projections[1].reshape(TOKENS, HEADS, HS).transpose(1, 0, 2)
    values = projections[2].reshape(TOKENS, HEADS, HS).transpose(1, 0, 2)
    positions = jnp.arange(TOKENS, dtype=jnp.int32)
    levels = (positions >= N0).astype(jnp.int32) + (positions >= N0 + N1).astype(jnp.int32)
    inv_root = 1.0 / HS ** 0.5

    def one_head(operands):
        head_queries, head_keys, head_values = operands
        key_wide = head_keys.astype(jnp.float32)
        value_wide = head_values.astype(jnp.float32)

        def one_block(block_index):
            first = (block_index * TOK_DEV).astype(jnp.int32)
            block_queries = lax.dynamic_slice_in_dim(head_queries, first, TOK_DEV, 0).astype(jnp.float32)
            block_levels = lax.dynamic_slice_in_dim(levels, first, TOK_DEV, 0)
            scores = jnp.dot(block_queries, key_wide.T) * inv_root
            allowed = levels[None, :] <= block_levels[:, None]
            row_max = lax.optimization_barrier(jnp.max(jnp.where(allowed, scores, -jnp.inf), axis=-1, keepdims=True))
            raw = jnp.where(allowed, jnp.exp(scores - row_max), 0.0)
            totals = lax.optimization_barrier(jnp.sum(raw, axis=-1, keepdims=True))
            weights = raw.astype(jnp.bfloat16).astype(jnp.float32)
            return jnp.dot(weights, value_wide) / totals
        blocks = lax.map(one_block, jnp.arange(N_SEQ, dtype=jnp.int32))
        return blocks.reshape(TOKENS, HS)
    attended = lax.map(one_head, (queries, keys, values))
    attended = attended.transpose(1, 0, 2).reshape(TOKENS, D).astype(jnp.bfloat16)
    mixed = (stream.astype(jnp.float32) + jnp.dot(attended, out_weight, preferred_element_type=jnp.float32)).astype(jnp.bfloat16)
    normed2 = rms_norm(mixed, norm_gain2)
    hidden = jax.nn.gelu(jnp.dot(normed2, up_weight, preferred_element_type=jnp.float32), approximate=True).astype(jnp.bfloat16)
    return (mixed.astype(jnp.float32) + jnp.dot(hidden, down_weight, preferred_element_type=jnp.float32)).astype(jnp.bfloat16)
```

```python
import functools

import jax
import jax.numpy as jnp
from jax import lax
from jax.experimental import pallas as pl
from jax.experimental.pallas import tpu as pltpu
from jax.sharding import PartitionSpec as P

D = 2048
HS = 128
C = 32
TOK = 336
FB = 256
HID = 512
FIRST = 512
SECOND = 2560
PARTS = 1
R = TOK // PARTS
MSG = R + 16
NCH = (R + 127) // 128
NZ = 8
KEYS = 8 * TOK
NEG = -1e30
QSCALE = 1.4426950408889634 / HS**0.5
MESH = pl.DeviceIdType.MESH
BF = jnp.bfloat16
F32 = jnp.float32
NT = (((1,), (1,)), ((), ()))


def split3(wide):
    high = wide.astype(BF)
    rest = wide - high.astype(F32)
    mid = rest.astype(BF)
    low = (rest - mid.astype(F32)).astype(BF)
    return high, mid, low


def level(token):
    return (token >= FIRST).astype(jnp.int32) + (token >= SECOND).astype(jnp.int32)


def halves(rows):
    first = (rows // 32) * 16
    return pl.ds(0, first), pl.ds(first, rows - first)


def kernel(
    cells_ref,
    pos_hbm,
    embed_hbm,
    gain1_ref,
    qkv_hbm,
    out_w_hbm,
    gain2_ref,
    up_hbm,
    down_hbm,
    out_ref,
    wqkv,
    wout,
    wup,
    wdown,
    grid_cells,
    pos_all,
    emb_all,
    inp,
    own_stream,
    acc,
    ssq,
    kv_send,
    q_send,
    kv_buf,
    q_buf,
    o_send,
    o_recv,
    state_o,
    state_m,
    attended,
    rs_send,
    rs_recv,
    mixed_all,
    acc2,
    ssq2,
    hidden,
    local_sem,
    cell_sem,
    pos_sem,
    emb_sem,
    kv_ssem,
    kv_rsem,
    q_ssem,
    q_rsem,
    o_ssem,
    o_rsem,
    rs_sem,
    mix_sem,
):
    seq = lax.axis_index("seq")
    z = lax.axis_index("head")
    x, y, c = seq // 8, lax.rem(seq // 2, 4), lax.rem(seq, 2)
    right, left = lax.rem(z + 1, NZ), lax.rem(z + NZ - 1, NZ)
    a0 = jnp.where(c == 0, x, y)
    b0 = jnp.where(c == 0, y, x)

    def sid(px, py, pc):
        return (px * 4 + py) * 2 + pc

    def ring(value, step):
        return lax.rem(value + step, 4)

    sibling = sid(x, y, 1 - c)

    loads = [
        pltpu.make_async_copy(pos_hbm.at[pl.ds(p * R, R)], pos_all.at[p, z], local_sem.at[p])
        for p in range(PARTS)
    ]
    loads.append(pltpu.make_async_copy(embed_hbm, emb_all.at[z], local_sem.at[PARTS]))
    weights = [
        pltpu.make_async_copy(src, dst, local_sem.at[PARTS + 1 + i])
        for i, (src, dst) in enumerate(
            ((qkv_hbm, wqkv), (out_w_hbm, wout), (up_hbm, wup), (down_hbm, wdown))
        )
    ]
    for load in loads:
        load.start()
    for load in weights:
        load.start()

    barrier = pltpu.get_barrier_semaphore()
    pl.semaphore_signal(barrier, inc=1, device_id={"head": right}, device_id_type=MESH)
    pl.semaphore_signal(barrier, inc=1, device_id={"head": left}, device_id_type=MESH)
    pl.semaphore_signal(barrier, inc=1, device_id={"seq": sibling}, device_id_type=MESH)
    for step in (1, 2, 3):
        for core in (0, 1):
            for peer in (sid(ring(x, step), y, core), sid(x, ring(y, step), core)):
                pl.semaphore_signal(barrier, inc=1, device_id={"seq": peer}, device_id_type=MESH)
    pl.semaphore_wait(barrier, 15)

    def remote(src, dst, ssem, rsem, **where):
        return pltpu.make_async_remote_copy(
            src_ref=src,
            dst_ref=dst,
            send_sem=ssem,
            recv_sem=rsem,
            device_id=where,
            device_id_type=MESH,
        )

    def ag_copies(buf, sems, rows, k):
        go, back = lax.rem(z + NZ - k, NZ), lax.rem(z + k, NZ)
        if k == 3:
            upper, lower = halves(rows)
        else:
            upper = lower = pl.ds(0, rows)
        return (
            remote(buf.at[go, upper], buf.at[go, upper], sems.at[0, k, 0], sems.at[0, k, 1], head=right),
            remote(buf.at[back, lower], buf.at[back, lower], sems.at[1, k, 0], sems.at[1, k, 1], head=left),
        )

    def ag_start(buf, sems, rows, k):
        for copy in ag_copies(buf, sems, rows, k):
            copy.start()

    def ag_wait(buf, sems, rows, k):
        for copy in ag_copies(buf, sems, rows, k):
            copy.wait_recv()

    def ag_drain(buf, sems, rows):
        for k in range(4):
            for copy in ag_copies(buf, sems, rows, k):
                copy.wait_send()

    pos_args = [(pos_all.at[p], pos_sem.at[p], R) for p in range(PARTS)]
    emb_args = (emb_all, emb_sem, C)
    mix_args = [(mixed_all.at[p], mix_sem.at[p], R) for p in range(PARTS)]

    for load in loads:
        load.wait()
    ag_start(*emb_args, 0)
    for p in range(PARTS):
        ag_start(*pos_args[p], 0)

    grid_cells[c, x, y] = cells_ref[...]
    along_y = [
        remote(
            grid_cells.at[c, x, y],
            grid_cells.at[c, x, y],
            cell_sem.at[step - 1, 0],
            cell_sem.at[step - 1, 1],
            seq=sid(x, ring(y, step), c),
        )
        for step in (1, 2, 3)
    ]
    for copy in along_y:
        copy.start()
    for copy in along_y:
        copy.wait_recv()
    along_x = [
        remote(
            grid_cells.at[c, x],
            grid_cells.at[c, x],
            cell_sem.at[2 + step, 0],
            cell_sem.at[2 + step, 1],
            seq=sid(ring(x, step), y, c),
        )
        for step in (1, 2, 3)
    ]
    for copy in along_x:
        copy.start()
    for copy in along_x:
        copy.wait_recv()
    across = remote(
        grid_cells.at[c], grid_cells.at[c], cell_sem.at[6, 0], cell_sem.at[6, 1], seq=sibling
    )
    across.start()

    token = seq * TOK + lax.broadcasted_iota(jnp.int32, (TOK, 1), 0)
    top, mid_level = token >= SECOND, token >= FIRST
    from_top, from_mid = token - SECOND, token - FIRST
    key_top = (from_top >> 8) * 64 + ((from_top & 127) >> 1)
    key_mid = (from_mid >> 7) * 32 + ((from_mid & 63) >> 1)
    fine_key = jnp.where(top, key_top, -1)
    coarse_key = jnp.where(top, -1, jnp.where(mid_level, key_mid, token))
    col = lax.broadcasted_iota(jnp.int32, (1, 2048), 1)
    cell_row = ((col >> 8) & 3) * 8 + ((col >> 6) & 3) * 2 + (col >> 10)
    cell_col = col & 63
    fine_col = cell_row * 64 + cell_col
    coarse_col = (cell_row >> 1) * 32 + (cell_col >> 1)
    select = jnp.where(
        fine_key == fine_col, 1.0, jnp.where(coarse_key == coarse_col, 0.25, 0.0)
    ).astype(BF)
    across.wait_recv()
    pooled = jnp.dot(
        select, grid_cells[...].reshape(2048, 128), preferred_element_type=F32
    )
    inputs = pooled[:, 0:C] + pooled[:, C : 2 * C] + pooled[:, 2 * C : 3 * C]
    for i, piece in enumerate(split3(inputs)):
        inp[i] = piece

    def embed_block(p, f, own=False):
        rows = pl.ds(p * R, R)
        emb = emb_all[f]
        wide = pos_all[p, f].astype(F32)
        for i in range(3):
            wide = wide + jnp.dot(inp[i, rows, :], emb, preferred_element_type=F32)
        stream = wide.astype(BF)
        if own:
            own_stream[rows, :] = stream
        wide = stream.astype(F32)
        square = wide * wide
        square = square[:, :128] + square[:, 128:]
        lanes = pl.ds(pl.multiple_of(f * FB, FB), FB)
        normed = (wide * gain1_ref[:, lanes]).astype(BF)
        for j in range(3):
            piece = jnp.dot(normed, wqkv[j, lanes, :], preferred_element_type=F32)
            if own:
                acc[rows, j * FB : (j + 1) * FB] = piece
            else:
                acc[rows, j * FB : (j + 1) * FB] += piece
        if own:
            ssq[rows, :] = square
        else:
            ssq[rows, :] += square

    def project(p):
        rows = pl.ds(p * R, R)
        total = jnp.sum(ssq[rows, :], axis=1, keepdims=True)
        scale = lax.rsqrt(total * (1.0 / D) + 1e-6)
        for h in range(2):
            cols = slice(h * HS, (h + 1) * HS)
            q_send[h, rows, :] = (acc[rows, cols] * (scale * QSCALE)).astype(BF)
            kv_send[h, rows, 0:HS] = (acc[rows, FB + h * HS : FB + (h + 1) * HS] * scale).astype(BF)
            kv_send[h, rows, HS:] = (
                acc[rows, 2 * FB + h * HS : 2 * FB + (h + 1) * HS] * scale
            ).astype(BF)

    def slot_rows(slot, p):
        return pl.ds(pl.multiple_of(slot * TOK + p * R, 16), R)

    def exchange(p):
        rows = pl.ds(p * R, R)
        kv_copies, q_copies = [], []

        def kv_copy(i, head, slot, dest):
            return remote(
                kv_send.at[head, rows],
                kv_buf.at[slot_rows(slot, p)],
                kv_ssem.at[p, i],
                kv_rsem.at[p, slot],
                seq=dest,
            )

        def q_copy(i, head, slot, dest):
            return remote(
                q_send.at[head, rows],
                q_buf.at[p, slot],
                q_ssem.at[p, i],
                q_rsem.at[p, slot],
                seq=dest,
            )

        other = 1 - c
        kv_copies.append(kv_copy(6, other, jnp.where(c == 1, x, y) * 2 + c, sibling))
        q_copies.append(q_copy(6, other, jnp.where(c == 1, y, x) * 2 + c, sibling))
        for i, step in enumerate((1, 3, 2)):
            kv_copies.append(kv_copy(i, 0, x * 2 + c, sid(ring(x, step), y, 0)))
            kv_copies.append(kv_copy(3 + i, 1, y * 2 + c, sid(x, ring(y, step), 1)))
            q_copies.append(q_copy(i, 0, y * 2 + c, sid(x, ring(y, step), 0)))
            q_copies.append(q_copy(3 + i, 1, x * 2 + c, sid(ring(x, step), y, 1)))
        return kv_copies, q_copies

    def exchange_start(p):
        rows = pl.ds(p * R, R)
        kv_copies, q_copies = exchange(p)
        for copy in q_copies + kv_copies:
            copy.start()
        kv_buf[slot_rows(a0 * 2 + c, p), :] = kv_send[c, rows, :]
        q_buf[p, b0 * 2 + c] = q_send[c, rows, :]

    def exchange_wait(p, want_q, want_kv):
        rows = pl.ds(p * R, R)
        for i in range(1, 8):
            if want_q:
                slot = lax.rem(b0 * 2 + c + i, 8)
                remote(
                    q_send.at[0, rows],
                    q_buf.at[p, slot],
                    q_ssem.at[p, 0],
                    q_rsem.at[p, slot],
                    seq=sibling,
                ).wait_recv()
            if want_kv:
                slot = lax.rem(a0 * 2 + c + i, 8)
                remote(
                    kv_send.at[0, rows],
                    kv_buf.at[slot_rows(slot, p)],
                    kv_ssem.at[p, 0],
                    kv_rsem.at[p, slot],
                    seq=sibling,
                ).wait_recv()

    def exchange_drain(p):
        kv_copies, q_copies = exchange(p)
        for copy in q_copies + kv_copies:
            copy.wait_send()

    ones_row = jnp.ones((1, HS), BF)

    def values_and_ones(kv):
        return jnp.concatenate([kv[:, HS:], jnp.broadcast_to(ones_row, (kv.shape[0], HS))], axis=1)

    diag = lax.broadcasted_iota(jnp.int32, (128, 128), 0) == lax.broadcasted_iota(
        jnp.int32, (128, 128), 1
    )

    def finish(p, first, count, total, largest):
        sums = total[:, HS:]
        sums = jnp.where(sums > 0.0, sums, 1.0)
        normal = (total[:, :HS] / sums).astype(BF)
        log_sum = largest + jnp.log2(sums)
        for i in range(count):
            o_send[p, first + i, 0:R, :] = normal[i * R : (i + 1) * R]
            lines = []
            for j in range(NCH):
                low, high = i * R + j * 128, i * R + min((j + 1) * 128, R)
                tile = log_sum[low:high]
                if high - low < 128:
                    tile = jnp.concatenate(
                        [tile, jnp.zeros((128 - (high - low), 128), F32)], axis=0
                    )
                lines.append(jnp.sum(jnp.where(diag, tile, 0.0), axis=0, keepdims=True))
            line = jnp.concatenate(lines, axis=0) if NCH > 1 else lines[0]
            high_part, mid_part, low_part = split3(line)
            packed = [v.astype(F32) for v in (high_part, mid_part, low_part)]
            packed.append(jnp.zeros((16 - 3 * NCH, 128), F32))
            o_send[p, first + i, R:MSG, :] = jnp.concatenate(packed, axis=0).astype(BF)

    KC = 896

    def full_tile(p, first, count):
        queries = q_buf[p, pl.ds(first, count)].reshape(count * R, HS)
        largest = total = None
        for j in range(KEYS // KC):
            kv = kv_buf[j * KC : (j + 1) * KC, :]
            scores = lax.dot_general(queries, kv[:, :HS], NT, preferred_element_type=F32)
            newest = jnp.max(scores, axis=1, keepdims=True)
            if total is not None:
                newest = jnp.maximum(newest, largest)
            weights = jnp.exp2(scores - newest).astype(BF)
            part = jnp.dot(weights, values_and_ones(kv), preferred_element_type=F32)
            total = part if total is None else total * jnp.exp2(largest - newest) + part
            largest = newest
        finish(p, first, count, total, largest)

    def masked_tile(p, b, first_q):
        rows = 2 * R
        first = b * 2
        state_m[...] = jnp.full((rows, 128), NEG, F32)
        state_o[...] = jnp.zeros((rows, 2 * HS), F32)
        line = lax.broadcasted_iota(jnp.int32, (rows, 1), 0)
        second = (line >= R).astype(jnp.int32)
        q_level = level((first_q + second) * TOK + p * R + line - second * R)
        top_level = level((first_q + 1) * TOK + TOK - 1)

        @pl.loop(0, 4)
        def _(a):
            first_k = jnp.where(c == 0, a * 8 + y * 2, x * 8 + a * 2)

            @pl.when(level(first_k * TOK) <= top_level)
            def _():
                kv = kv_buf[pl.ds(pl.multiple_of(a * 2 * TOK, 16), 2 * TOK), :]
                queries = q_buf[p, pl.ds(first, 2)].reshape(rows, HS)
                scores = lax.dot_general(queries, kv[:, :HS], NT, preferred_element_type=F32)
                k_level = level(
                    first_k * TOK + lax.broadcasted_iota(jnp.int32, (1, 2 * TOK), 1)
                )
                scores = jnp.where(k_level <= q_level, scores, NEG)
                before = state_m[:, 0:1]
                newest = jnp.maximum(before, jnp.max(scores, axis=1, keepdims=True))
                weights = jnp.exp2(scores - newest).astype(BF)
                part = jnp.dot(weights, values_and_ones(kv), preferred_element_type=F32)
                state_o[...] = state_o[...] * jnp.exp2(before - newest) + part
                state_m[...] = jnp.broadcast_to(newest, (rows, 128))

        finish(p, first, 2, state_o[...], state_m[:, 0:1])

    def attend(p):
        everything = jnp.logical_and(c == 0, x >= 1)

        @pl.when(everything)
        def _():
            @pl.loop(0, 2)
            def _(i):
                full_tile(p, i * 4, 2)
                full_tile(p, i * 4 + 2, 2)

        @pl.when(jnp.logical_not(everything))
        def _():
            @pl.loop(0, 4)
            def _(b):
                first_q = jnp.where(c == 0, x * 8 + b * 2, b * 8 + y * 2)
                plain = first_q >= 8

                @pl.when(plain)
                def _():
                    full_tile(p, b * 2, 2)

                @pl.when(jnp.logical_not(plain))
                def _():
                    masked_tile(p, b, first_q)

    def give_copies(p):
        copies = [
            remote(
                o_send.at[p, b0 * 2 + 1 - c],
                o_recv.at[p, c * 4 + b0],
                o_ssem.at[p, 6],
                o_rsem.at[p, c * 4 + b0],
                seq=sibling,
            )
        ]
        for i, step in enumerate((1, 3, 2)):
            b = ring(b0, step)
            for core in (0, 1):
                dest = jnp.where(c == 0, sid(x, b, core), sid(b, y, core))
                copies.append(
                    remote(
                        o_send.at[p, b * 2 + core],
                        o_recv.at[p, c * 4 + b0],
                        o_ssem.at[p, i * 2 + core],
                        o_rsem.at[p, c * 4 + b0],
                        seq=dest,
                    )
                )
        return copies

    def give_start(p):
        for copy in give_copies(p):
            copy.start()
        o_recv[p, c * 4 + b0] = o_send[p, b0 * 2 + c]

    def give_wait(p):
        for i in range(1, 8):
            slot = lax.rem(c * 4 + b0 + i, 8)
            remote(
                o_send.at[p, 0],
                o_recv.at[p, slot],
                o_ssem.at[p, 0],
                o_rsem.at[p, slot],
                seq=sibling,
            ).wait_recv()

    def give_drain(p):
        for copy in give_copies(p):
            copy.wait_send()

    def combine(p):
        tails = [o_recv[p, i, R:MSG, :].astype(F32) for i in range(8)]
        for j in range(NCH):
            low, high = j * 128, min((j + 1) * 128, R)
            logs = [
                t[j : j + 1] + t[NCH + j : NCH + j + 1] + t[2 * NCH + j : 2 * NCH + j + 1]
                for t in tails
            ]
            shares = []
            for h in range(2):
                four = logs[h * 4 : h * 4 + 4]
                largest = functools.reduce(jnp.maximum, four)
                powers = [jnp.exp2(v - largest) for v in four]
                total = powers[0] + powers[1] + powers[2] + powers[3]
                shares += [v / total for v in powers]
            for h in range(2):
                mean = None
                for a in range(4):
                    share = jnp.sum(
                        jnp.where(diag, shares[h * 4 + a], 0.0), axis=1, keepdims=True
                    )
                    term = o_recv[p, h * 4 + a, low:high, :].astype(F32) * share[: high - low]
                    mean = term if mean is None else mean + term
                attended[p * R + low : p * R + high, h * HS : (h + 1) * HS] = mean.astype(BF)

    def rs_copies(p, phase, k):
        upper, lower = halves(R)
        if k > 0:
            upper = lower = pl.ds(0, R)
        send, recv, sems = rs_send.at[phase, p], rs_recv.at[phase, p], rs_sem.at[phase, p]
        return (
            remote(send.at[0, k, upper], recv.at[0, k, upper], sems.at[0, k, 0], sems.at[0, k, 1], head=right),
            remote(send.at[1, k, lower], recv.at[1, k, lower], sems.at[1, k, 0], sems.at[1, k, 1], head=left),
        )

    def rs_step(p, phase, block, k):
        upper, lower = halves(R)
        send, recv = rs_send.at[phase, p], rs_recv.at[phase, p]
        if k == 0:
            term = block(lax.rem(z + 4, NZ)).astype(BF)
            send[0, 0, upper, :] = term[upper.start : upper.start + upper.size]
            send[1, 0, lower, :] = term[lower.start : lower.start + lower.size]
            for copy in rs_copies(p, phase, 0):
                copy.start()
            return
        ahead = block(lax.rem(z + 4 - k, NZ))
        behind = block(lax.rem(z + 4 + k, NZ))
        go, back = rs_copies(p, phase, k - 1)
        go_next, back_next = rs_copies(p, phase, k)
        go.wait_recv()
        if k == 1:
            n = upper.size
            send[0, k, upper, :] = (ahead[:n] + recv[0, 0, upper, :].astype(F32)).astype(BF)
            send[0, k, lower, :] = ahead[n:].astype(BF)
        else:
            send[0, k] = (ahead + recv[0, k - 1].astype(F32)).astype(BF)
        go_next.start()
        back.wait_recv()
        if k == 1:
            send[1, k, upper, :] = behind[:n].astype(BF)
            send[1, k, lower, :] = (behind[n:] + recv[1, 0, lower, :].astype(F32)).astype(BF)
        else:
            send[1, k] = (behind + recv[1, k - 1].astype(F32)).astype(BF)
        back_next.start()

    def rs_end(p, phase, block):
        own = block(z)
        go, back = rs_copies(p, phase, 3)
        go.wait_recv()
        back.wait_recv()
        recv = rs_recv.at[phase, p]
        return own + recv[0, 3].astype(F32) + recv[1, 3].astype(F32)

    def rs_drain(p, phase):
        for k in range(4):
            for copy in rs_copies(p, phase, k):
                copy.wait_send()

    def out_block(p):
        def block(f):
            lanes = pl.ds(pl.multiple_of(f * FB, FB), FB)
            return jnp.dot(
                attended[p * R : (p + 1) * R, :], wout[:, lanes], preferred_element_type=F32
            )

        return block

    def down_block(p):
        def block(f):
            lanes = pl.ds(pl.multiple_of(f * FB, FB), FB)
            return jnp.dot(
                hidden[p * R : (p + 1) * R, :], wdown[:, lanes], preferred_element_type=F32
            )

        return block

    def mix(p):
        rows = pl.ds(p * R, R)
        summed = rs_end(p, 0, out_block(p))
        mixed_all[p, z] = (own_stream[rows, :].astype(F32) + summed).astype(BF)

    def up_part(p, f, own=False):
        rows = pl.ds(p * R, R)
        wide = mixed_all[p, f].astype(F32)
        square = wide * wide
        square = square[:, :128] + square[:, 128:]
        lanes = pl.ds(pl.multiple_of(f * FB, FB), FB)
        normed = (wide * gain2_ref[:, lanes]).astype(BF)
        piece = jnp.dot(normed, wup[lanes, :], preferred_element_type=F32)
        if own:
            acc2[rows, :] = piece
            ssq2[rows, :] = square
        else:
            acc2[rows, :] += piece
            ssq2[rows, :] += square

    def activate(p):
        rows = pl.ds(p * R, R)
        total = jnp.sum(ssq2[rows, :], axis=1, keepdims=True)
        scale = lax.rsqrt(total * (1.0 / D) + 1e-6)
        hidden[rows, :] = jax.nn.gelu(acc2[rows, :] * scale, approximate=True).astype(BF)

    def last(p):
        rows = pl.ds(p * R, R)
        summed = rs_end(p, 1, down_block(p))
        out_ref[rows, :] = (mixed_all[p, z].astype(F32) + summed).astype(BF)

    weights[0].wait()
    for p in range(PARTS):
        embed_block(p, z, own=True)
    for k in range(4):
        ag_wait(*emb_args, k)
        if k < 3:
            ag_start(*emb_args, k + 1)
        for p in range(PARTS):
            ag_wait(*pos_args[p], k)
            if k < 3:
                ag_start(*pos_args[p], k + 1)
            embed_block(p, lax.rem(z + NZ - 1 - k, NZ))
            if k < 3:
                embed_block(p, lax.rem(z + 1 + k, NZ))
    for p in range(PARTS):
        project(p)
        exchange_start(p)
    for p in range(PARTS):
        exchange_wait(p, True, True)
    for p in range(PARTS):
        attend(p)
        give_start(p)
    weights[1].wait()
    for p in range(PARTS):
        give_wait(p)
        combine(p)
    for k in range(4):
        for p in range(PARTS):
            rs_step(p, 0, out_block(p), k)
    weights[2].wait()
    weights[3].wait()
    for p in range(PARTS):
        mix(p)
        ag_start(*mix_args[p], 0)
        up_part(p, z, own=True)
    for k in range(4):
        for p in range(PARTS):
            ag_wait(*mix_args[p], k)
            if k < 3:
                ag_start(*mix_args[p], k + 1)
            up_part(p, lax.rem(z + NZ - 1 - k, NZ))
            if k < 3:
                up_part(p, lax.rem(z + 1 + k, NZ))
    for p in range(PARTS):
        activate(p)
    for k in range(4):
        for p in range(PARTS):
            rs_step(p, 1, down_block(p), k)
    for p in range(PARTS):
        last(p)

    for copy in along_y + along_x + [across]:
        copy.wait_send()
    ag_drain(*emb_args)
    for p in range(PARTS):
        ag_drain(*pos_args[p])
        exchange_drain(p)
        give_drain(p)
        rs_drain(p, 0)
        ag_drain(*mix_args[p])
        rs_drain(p, 1)


def pool_cells(latent):
    pixels = latent.reshape(2, 64, 2, C).astype(jnp.float32)
    pooled = (pixels[0, :, 0] + pixels[0, :, 1] + pixels[1, :, 0] + pixels[1, :, 1]) * 0.25
    high = lax.reduce_precision(pooled, 8, 7)
    mid = lax.reduce_precision(pooled - high, 8, 7)
    low = pooled - high - mid
    return jnp.concatenate([high, mid, low, jnp.zeros_like(low)], axis=1).astype(BF)


def body(latent, pos, embed, gain1, qkv_w, out_w, gain2, up, down):
    vmem = pl.BlockSpec(memory_space=pltpu.VMEM)
    hbm = pl.BlockSpec(memory_space=pl.ANY)
    dma = pltpu.SemaphoreType.DMA
    return pl.pallas_call(
        kernel,
        out_shape=jax.ShapeDtypeStruct((TOK, FB), BF),
        in_specs=[vmem, hbm, hbm, vmem, hbm, hbm, vmem, hbm, hbm],
        out_specs=vmem,
        scratch_shapes=[
            pltpu.VMEM((3, D, FB), BF),
            pltpu.VMEM((FB, D), BF),
            pltpu.VMEM((D, HID), BF),
            pltpu.VMEM((HID, D), BF),
            pltpu.VMEM((2, 4, 4, 64, 128), BF),
            pltpu.VMEM((PARTS, NZ, R, FB), BF),
            pltpu.VMEM((NZ, C, FB), BF),
            pltpu.VMEM((3, TOK, C), BF),
            pltpu.VMEM((TOK, FB), BF),
            pltpu.VMEM((TOK, 3 * FB), F32),
            pltpu.VMEM((TOK, 128), F32),
            pltpu.VMEM((2, TOK, 2 * HS), BF),
            pltpu.VMEM((2, TOK, HS), BF),
            pltpu.VMEM((KEYS, 2 * HS), BF),
            pltpu.VMEM((PARTS, 8, R, HS), BF),
            pltpu.VMEM((PARTS, 8, MSG, HS), BF),
            pltpu.VMEM((PARTS, 8, MSG, HS), BF),
            pltpu.VMEM((2 * R, 2 * HS), F32),
            pltpu.VMEM((2 * R, 128), F32),
            pltpu.VMEM((TOK, FB), BF),
            pltpu.VMEM((2, PARTS, 2, 4, R, FB), BF),
            pltpu.VMEM((2, PARTS, 2, 4, R, FB), BF),
            pltpu.VMEM((PARTS, NZ, R, FB), BF),
            pltpu.VMEM((TOK, HID), F32),
            pltpu.VMEM((TOK, 128), F32),
            pltpu.VMEM((TOK, HID), BF),
            dma((PARTS + 5,)),
            dma((7, 2)),
            dma((PARTS, 2, 4, 2)),
            dma((2, 4, 2)),
            dma((PARTS, 7)),
            dma((PARTS, 8)),
            dma((PARTS, 7)),
            dma((PARTS, 8)),
            dma((PARTS, 7)),
            dma((PARTS, 8)),
            dma((2, PARTS, 2, 4, 2)),
            dma((PARTS, 2, 4, 2)),
        ],
        compiler_params=pltpu.CompilerParams(
            collective_id=0, has_side_effects=True, vmem_limit_bytes=56 * 2**20
        ),
    )(
        pool_cells(latent),
        pos,
        embed,
        gain1.reshape(1, D),
        qkv_w,
        out_w,
        gain2.reshape(1, D),
        up,
        down,
    )


def solution(mesh):
    in_specs = (
        P("seq", None),
        P("seq", "head"),
        P(None, "head"),
        P(),
        P(None, None, "head"),
        P("head", None),
        P(),
        P(None, "head"),
        P("head", None),
    )
    return jax.shard_map(
        body, mesh=mesh, in_specs=in_specs, out_specs=P("seq", "head"), check_vma=False
    )
```

```python
import functools

import jax
import jax.numpy as jnp
from jax import lax
from jax.experimental import pallas as pl
from jax.experimental.pallas import tpu as pltpu
from jax.sharding import PartitionSpec as P

D = 2048
HS = 128
C = 32
TOK = 336
FB = 256
HID = 512
FIRST = 512
SECOND = 2560
PARTS = 3
R = TOK // PARTS
MSG = R + 16
NZ = 8
KEYS = 8 * TOK
NEG = -1e30
QSCALE = 1.4426950408889634 / HS**0.5
MESH = pl.DeviceIdType.MESH
BF = jnp.bfloat16
F32 = jnp.float32
NT = (((1,), (1,)), ((), ()))


def split3(wide):
    high = wide.astype(BF)
    rest = wide - high.astype(F32)
    mid = rest.astype(BF)
    low = (rest - mid.astype(F32)).astype(BF)
    return high, mid, low


def level(token):
    return (token >= FIRST).astype(jnp.int32) + (token >= SECOND).astype(jnp.int32)


def halves(rows, p):
    first = ((rows // 16 + p % 2) // 2) * 16
    return pl.ds(0, first), pl.ds(first, rows - first)


def kernel(
    latent_ref,
    pos_hbm,
    embed_hbm,
    gain1_ref,
    qkv_hbm,
    out_w_hbm,
    gain2_ref,
    up_hbm,
    down_hbm,
    out_ref,
    wqkv,
    wout,
    wup,
    wdown,
    grid_cells,
    pos_all,
    emb_all,
    select,
    lines_buf,
    inp,
    own_stream,
    acc,
    ssq,
    kv_send,
    q_send,
    kv_buf,
    q_buf,
    o_send,
    o_recv,
    state_o,
    state_m,
    attended,
    rs_send,
    rs_recv,
    mixed_all,
    acc2,
    ssq2,
    hidden,
    local_sem,
    cell_ssem,
    cell_rsem,
    pos_sem,
    emb_sem,
    kv_ssem,
    kv_rsem,
    q_ssem,
    q_rsem,
    o_ssem,
    o_rsem,
    rs_sem,
    mix_sem,
):
    seq = lax.axis_index("seq")
    z = lax.axis_index("head")
    x, y, c = seq >> 3, (seq >> 1) & 3, seq & 1
    right, left = (z + 1) & 7, (z + 7) & 7
    a0 = jnp.where(c == 0, x, y)
    b0 = jnp.where(c == 0, y, x)

    def sid(px, py, pc):
        return (px * 4 + py) * 2 + pc

    def ring(value, step):
        return (value + step) & 3

    sibling = sid(x, y, 1 - c)

    loads = [
        pltpu.make_async_copy(pos_hbm, pos_all.at[z], local_sem.at[0])
    ]
    loads.append(pltpu.make_async_copy(embed_hbm, emb_all.at[z], local_sem.at[1]))
    weights = [
        pltpu.make_async_copy(src, dst, local_sem.at[2 + i])
        for i, (src, dst) in enumerate(
            ((qkv_hbm, wqkv), (out_w_hbm, wout), (up_hbm, wup), (down_hbm, wdown))
        )
    ]
    for load in loads:
        load.start()
    for load in weights:
        load.start()

    wide = latent_ref[...].astype(F32)
    both = wide[0:1] + wide[1:2]
    for j in range(32):
        lines_buf[j : j + 1, :] = both[:, j * 128 : (j + 1) * 128]
    wide = lines_buf[...] * 0.25
    pooled = jnp.concatenate(
        [wide[:, 0:C] + wide[:, C : 2 * C], wide[:, 2 * C : 3 * C] + wide[:, 3 * C :]], axis=0
    )
    grid_cells[...] = jnp.zeros((32, 64, 128), BF)
    grid_cells[seq] = jnp.concatenate([*split3(pooled), jnp.zeros((64, C), BF)], axis=1)

    token = seq * TOK + lax.broadcasted_iota(jnp.int32, (TOK, 1), 0)
    top, mid_level = token >= SECOND, token >= FIRST
    from_top, from_mid = token - SECOND, token - FIRST
    key_top = (from_top >> 8) * 64 + ((from_top & 127) >> 1)
    key_mid = (from_mid >> 7) * 32 + ((from_mid & 63) >> 1)
    fine_key = jnp.where(top, key_top, -1)
    coarse_key = jnp.where(top, -1, jnp.where(mid_level, key_mid, token))
    col = lax.broadcasted_iota(jnp.int32, (1, 2048), 1)
    cell_row, cell_col = col >> 6, (col & 31) * 2 + ((col >> 5) & 1)
    fine_col = cell_row * 64 + cell_col
    coarse_col = (cell_row >> 1) * 32 + (cell_col >> 1)
    select[...] = jnp.where(
        fine_key == fine_col, 1.0, jnp.where(coarse_key == coarse_col, 0.25, 0.0)
    ).astype(BF)

    barrier = pltpu.get_barrier_semaphore()
    pl.semaphore_signal(barrier, inc=1, device_id={"head": right}, device_id_type=MESH)
    pl.semaphore_signal(barrier, inc=1, device_id={"head": left}, device_id_type=MESH)
    for step in range(1, 32):
        peer = (seq + step) & 31
        pl.semaphore_signal(barrier, inc=1, device_id={"seq": peer}, device_id_type=MESH)
    pl.semaphore_wait(barrier, 33)

    def remote(src, dst, ssem, rsem, **where):
        return pltpu.make_async_remote_copy(
            src_ref=src,
            dst_ref=dst,
            send_sem=ssem,
            recv_sem=rsem,
            device_id=where,
            device_id_type=MESH,
        )

    def ag_copies(buf, sems, base, rows, p, k):
        go, back = (z - k) & 7, (z + k) & 7
        if k == 3:
            upper, lower = halves(rows, p)
            upper = pl.ds(base + upper.start, upper.size)
            lower = pl.ds(base + lower.start, lower.size)
        else:
            upper = lower = pl.ds(base, rows)
        return (
            remote(buf.at[go, upper], buf.at[go, upper], sems.at[0, k, 0], sems.at[0, k, 1], head=right),
            remote(buf.at[back, lower], buf.at[back, lower], sems.at[1, k, 0], sems.at[1, k, 1], head=left),
        )

    def ag_start(*args):
        for copy in ag_copies(*args):
            copy.start()

    def ag_wait(*args):
        for copy in ag_copies(*args):
            copy.wait_recv()

    def ag_drain(*args):
        for k in range(4):
            for copy in ag_copies(*args, k):
                copy.wait_send()

    pos_args = [(pos_all, pos_sem.at[p], p * R, R, p) for p in range(PARTS)]
    emb_args = (emb_all, emb_sem, 0, C, 0)
    mix_args = [(mixed_all.at[p], mix_sem.at[p], 0, R, p) for p in range(PARTS)]

    for load in loads:
        load.wait()
    ag_start(*emb_args, 0)
    for p in range(PARTS):
        ag_start(*pos_args[p], 0)

    def takers(row):
        fine, coarse = SECOND + 256 * row, row >> 1
        middle, low = FIRST + 128 * coarse, 32 * coarse
        return (fine, fine + 255), (middle, middle + 127), (low, low + 31)

    def owner(token):
        return (token * 49933) >> 24

    def cell_copy(i, row, dest):
        return remote(
            grid_cells.at[row], grid_cells.at[row], cell_ssem.at[i], cell_rsem.at[row], seq=dest
        )

    def each_taker(act):
        for i, ends in enumerate(takers(seq)):
            one, two = owner(ends[0]), owner(ends[1])

            @pl.when(one != seq)
            def _():
                act(cell_copy(2 * i, seq, one))

            @pl.when(jnp.logical_and(two != one, two != seq))
            def _():
                act(cell_copy(2 * i + 1, seq, two))

    each_taker(lambda copy: copy.start())

    def wait_cells():
        start, end = seq * TOK, seq * TOK + TOK - 1

        def wait_rows(low, high):
            @pl.loop(low, high)
            def _(row):
                @pl.when(row != seq)
                def _():
                    cell_copy(0, row, sibling).wait_recv()

        @pl.when(end >= SECOND)
        def _():
            wait_rows(jnp.maximum(start - SECOND, 0) >> 8, ((end - SECOND) >> 8) + 1)

        @pl.when(jnp.logical_and(end >= FIRST, start < SECOND))
        def _():
            wait_rows(
                (jnp.maximum(start - FIRST, 0) >> 7) * 2,
                ((jnp.minimum(end, SECOND - 1) - FIRST) >> 7) * 2 + 2,
            )

        @pl.when(start < FIRST)
        def _():
            wait_rows((start >> 5) * 2, (jnp.minimum(end, FIRST - 1) >> 5) * 2 + 2)

    def pool_inputs():
        pooled = jnp.dot(
            select[...], grid_cells[...].reshape(2048, 128), preferred_element_type=F32
        )
        inputs = pooled[:, 0:C] + pooled[:, C : 2 * C] + pooled[:, 2 * C : 3 * C]
        for i, piece in enumerate(split3(inputs)):
            inp[i] = piece

    def group_rows(p):
        return pl.ds(p * R, R)

    def embed_block(g, f, own=False):
        rows = group_rows(g)
        emb = emb_all[f]
        wide = pos_all[f, rows, :].astype(F32)
        for i in range(3):
            wide = wide + jnp.dot(inp[i, rows, :], emb, preferred_element_type=F32)
        stream = wide.astype(BF)
        if own:
            own_stream[rows, :] = stream
        wide = stream.astype(F32)
        square = wide * wide
        square = square[:, :128] + square[:, 128:]
        lanes = pl.ds(pl.multiple_of(f * FB, FB), FB)
        normed = (wide * gain1_ref[:, lanes]).astype(BF)
        for j in range(3):
            piece = jnp.dot(normed, wqkv[j, lanes, :], preferred_element_type=F32)
            if own:
                acc[rows, j * FB : (j + 1) * FB] = piece
            else:
                acc[rows, j * FB : (j + 1) * FB] += piece
        if own:
            ssq[rows, :] = square
        else:
            ssq[rows, :] += square

    def project(g):
        rows = group_rows(g)
        total = jnp.sum(ssq[rows, :], axis=1, keepdims=True)
        scale = lax.rsqrt(total * (1.0 / D) + 1e-6)
        for h in range(2):
            cols = slice(h * HS, (h + 1) * HS)
            q_send[h, rows, :] = (acc[rows, cols] * (scale * QSCALE)).astype(BF)
            kv_send[h, rows, 0:HS] = (acc[rows, FB + h * HS : FB + (h + 1) * HS] * scale).astype(BF)
            kv_send[h, rows, HS:] = (
                acc[rows, 2 * FB + h * HS : 2 * FB + (h + 1) * HS] * scale
            ).astype(BF)

    def slot_rows(slot, g):
        return pl.ds(pl.multiple_of(slot * TOK + g * R, 16), R)

    def exchange(p):
        rows = group_rows(p)
        kv_copies, q_copies = [], []

        def kv_copy(i, head, slot, dest):
            return remote(
                kv_send.at[head, rows],
                kv_buf.at[slot_rows(slot, p)],
                kv_ssem.at[p, i],
                kv_rsem.at[p, slot],
                seq=dest,
            )

        def q_copy(i, head, slot, dest):
            return remote(
                q_send.at[head, rows],
                q_buf.at[slot_rows(slot, p)],
                q_ssem.at[p, i],
                q_rsem.at[p, slot],
                seq=dest,
            )

        other = 1 - c
        kv_copies.append(kv_copy(6, other, jnp.where(c == 1, x, y) * 2 + c, sibling))
        q_copies.append(q_copy(6, other, jnp.where(c == 1, y, x) * 2 + c, sibling))
        for i, step in enumerate((1, 3, 2)):
            kv_copies.append(kv_copy(i, 0, x * 2 + c, sid(ring(x, step), y, 0)))
            kv_copies.append(kv_copy(3 + i, 1, y * 2 + c, sid(x, ring(y, step), 1)))
            q_copies.append(q_copy(i, 0, y * 2 + c, sid(x, ring(y, step), 0)))
            q_copies.append(q_copy(3 + i, 1, x * 2 + c, sid(ring(x, step), y, 1)))
        return kv_copies, q_copies

    def exchange_start(p):
        rows = group_rows(p)
        kv_copies, q_copies = exchange(p)
        for copy in q_copies + kv_copies:
            copy.start()
        kv_buf[slot_rows(a0 * 2 + c, p), :] = kv_send[c, rows, :]
        q_buf[slot_rows(b0 * 2 + c, p), :] = q_send[c, rows, :]

    def exchange_wait(p, want_q, want_kv):
        rows = group_rows(p)
        for i in range(1, 8):
            if want_q:
                slot = (b0 * 2 + c + i) & 7
                remote(
                    q_send.at[0, rows],
                    q_buf.at[slot_rows(slot, p)],
                    q_ssem.at[p, 0],
                    q_rsem.at[p, slot],
                    seq=sibling,
                ).wait_recv()
            if want_kv:
                slot = (a0 * 2 + c + i) & 7
                remote(
                    kv_send.at[0, rows],
                    kv_buf.at[slot_rows(slot, p)],
                    kv_ssem.at[p, 0],
                    kv_rsem.at[p, slot],
                    seq=sibling,
                ).wait_recv()

    def exchange_drain(p):
        kv_copies, q_copies = exchange(p)
        for copy in q_copies + kv_copies:
            copy.wait_send()

    ones_row = jnp.ones((1, HS), BF)

    def values_and_ones(kv):
        return jnp.concatenate([kv[:, HS:], jnp.broadcast_to(ones_row, (kv.shape[0], HS))], axis=1)

    diag = lax.broadcasted_iota(jnp.int32, (128, 128), 0) == lax.broadcasted_iota(
        jnp.int32, (128, 128), 1
    )

    def finish(slot, total, largest):
        sums = total[:, HS:]
        normal = (total[:, :HS] / sums).astype(BF)
        log_sum = largest + jnp.log2(sums)
        for p in range(PARTS):
            low = p * R
            o_send[p, slot, 0:R, :] = normal[low : low + R]
            tile = jnp.concatenate(
                [log_sum[low : low + R], jnp.zeros((128 - R, 128), F32)], axis=0
            )
            line = jnp.sum(jnp.where(diag, tile, 0.0), axis=0, keepdims=True)
            packed = [v.astype(F32) for v in split3(line)] + [jnp.zeros((13, 128), F32)]
            o_send[p, slot, R:MSG, :] = jnp.concatenate(packed, axis=0).astype(BF)

    CHUNK = 896

    def plain_slot(slot):
        queries = q_buf[pl.ds(pl.multiple_of(slot * TOK, 16), TOK), :]
        largest = total = None
        for low in range(0, KEYS, CHUNK):
            kv = kv_buf[low : low + CHUNK, :]
            scores = lax.dot_general(queries, kv[:, :HS], NT, preferred_element_type=F32)
            newest = jnp.max(scores, axis=1, keepdims=True)
            if total is not None:
                newest = jnp.maximum(newest, largest)
            weights = jnp.exp2(scores - newest).astype(BF)
            part = jnp.dot(weights, values_and_ones(kv), preferred_element_type=F32)
            total = part if total is None else total * jnp.exp2(largest - newest) + part
            largest = newest
        finish(slot, total, largest)

    def masked_slot(slot, chunks):
        b, core = slot >> 1, slot & 1
        first_q = jnp.where(c == 0, x * 8 + b * 2, b * 8 + y * 2) + core
        q_level = level(first_q * TOK + lax.broadcasted_iota(jnp.int32, (TOK, 1), 0))
        state_m[...] = jnp.full((TOK, 128), NEG, F32)
        state_o[...] = jnp.zeros((TOK, 2 * HS), F32)

        @pl.loop(0, chunks)
        def _(i):
            low = pl.multiple_of(i * CHUNK, 128)
            kv = kv_buf[pl.ds(low, CHUNK), :]
            queries = q_buf[pl.ds(pl.multiple_of(slot * TOK, 16), TOK), :]
            scores = lax.dot_general(queries, kv[:, :HS], NT, preferred_element_type=F32)
            key = low + lax.broadcasted_iota(jnp.int32, (1, CHUNK), 1)
            block = sum((key >= edge * 2 * TOK).astype(jnp.int32) for edge in (1, 2, 3))
            shift = jnp.where(c == 0, block * (6 * TOK) + y * 2 * TOK, x * 8 * TOK)
            scores = jnp.where(level(key + shift) <= q_level, scores, NEG)
            before = state_m[:, 0:1]
            newest = jnp.maximum(before, jnp.max(scores, axis=1, keepdims=True))
            weights = jnp.exp2(scores - newest).astype(BF)
            part = jnp.dot(weights, values_and_ones(kv), preferred_element_type=F32)
            state_o[...] = state_o[...] * jnp.exp2(before - newest) + part
            state_m[...] = jnp.broadcast_to(newest, (TOK, 128))

        finish(slot, state_o[...], state_m[:, 0:1])

    def attend():
        first_plain = jnp.where(c == 0, jnp.where(x == 0, 4, 0), 1)

        @pl.loop(first_plain, 4)
        def _(b):
            plain_slot(b * 2)
            plain_slot(b * 2 + 1)

        nothing = jnp.logical_and(c == 1, jnp.logical_and(x >= 1, y < 3))

        @pl.when(nothing)
        def _():
            for i in range(2):
                for p in range(PARTS):
                    o_send[p, i, 0:R, :] = jnp.zeros((R, HS), BF)
                    o_send[p, i, R:MSG, :] = jnp.full((MSG - R, HS), NEG, BF)

        @pl.when(jnp.logical_not(nothing))
        def _():
            @pl.loop(0, first_plain * 2)
            def _(slot):
                masked_slot(slot, jnp.where(jnp.logical_and(c == 0, slot < 7), 1, 3))

    def give_copies(p):
        copies = [
            remote(
                o_send.at[p, b0 * 2 + 1 - c],
                o_recv.at[p, c * 4 + b0],
                o_ssem.at[p, 6],
                o_rsem.at[p, c * 4 + b0],
                seq=sibling,
            )
        ]
        for i, step in enumerate((1, 3, 2)):
            b = ring(b0, step)
            for core in (0, 1):
                dest = jnp.where(c == 0, sid(x, b, core), sid(b, y, core))
                copies.append(
                    remote(
                        o_send.at[p, b * 2 + core],
                        o_recv.at[p, c * 4 + b0],
                        o_ssem.at[p, i * 2 + core],
                        o_rsem.at[p, c * 4 + b0],
                        seq=dest,
                    )
                )
        return copies

    def give_start(p):
        for copy in give_copies(p):
            copy.start()
        o_recv[p, c * 4 + b0] = o_send[p, b0 * 2 + c]

    def give_wait(p):
        for i in range(1, 8):
            slot = (c * 4 + b0 + i) & 7
            remote(
                o_send.at[p, 0],
                o_recv.at[p, slot],
                o_ssem.at[p, 0],
                o_rsem.at[p, slot],
                seq=sibling,
            ).wait_recv()

    def give_drain(p):
        for copy in give_copies(p):
            copy.wait_send()

    def combine(p):
        tails = [o_recv[p, i, R:MSG, :].astype(F32) for i in range(8)]
        logs = [t[0:1] + t[1:2] + t[2:3] for t in tails]
        for h in range(2):
            four = logs[h * 4 : h * 4 + 4]
            largest = functools.reduce(jnp.maximum, four)
            powers = [jnp.exp2(v - largest) for v in four]
            total = powers[0] + powers[1] + powers[2] + powers[3]
            mean = None
            for a in range(4):
                share = jnp.sum(
                    jnp.where(diag, powers[a] / total, 0.0), axis=1, keepdims=True
                )
                term = o_recv[p, h * 4 + a, 0:R, :].astype(F32) * share[:R]
                mean = term if mean is None else mean + term
            attended[p * R : (p + 1) * R, h * HS : (h + 1) * HS] = mean.astype(BF)

    def rs_copies(p, phase, k):
        upper, lower = halves(R, p)
        if k > 0:
            upper = lower = pl.ds(0, R)
        send, recv, sems = rs_send.at[phase, p], rs_recv.at[phase, p], rs_sem.at[phase, p]
        return (
            remote(send.at[0, k, upper], recv.at[0, k, upper], sems.at[0, k, 0], sems.at[0, k, 1], head=right),
            remote(send.at[1, k, lower], recv.at[1, k, lower], sems.at[1, k, 0], sems.at[1, k, 1], head=left),
        )

    def rs_step(p, phase, block, k):
        upper, lower = halves(R, p)
        send, recv = rs_send.at[phase, p], rs_recv.at[phase, p]
        if k == 0:
            term = block((z + 4) & 7).astype(BF)
            send[0, 0, upper, :] = term[upper.start : upper.start + upper.size]
            send[1, 0, lower, :] = term[lower.start : lower.start + lower.size]
            for copy in rs_copies(p, phase, 0):
                copy.start()
            return
        ahead = block((z + 4 - k) & 7)
        behind = block((z + 4 + k) & 7)
        go, back = rs_copies(p, phase, k - 1)
        go_next, back_next = rs_copies(p, phase, k)
        go.wait_recv()
        if k == 1:
            n = upper.size
            send[0, k, upper, :] = (ahead[:n] + recv[0, 0, upper, :].astype(F32)).astype(BF)
            send[0, k, lower, :] = ahead[n:].astype(BF)
        else:
            send[0, k] = (ahead + recv[0, k - 1].astype(F32)).astype(BF)
        go_next.start()
        back.wait_recv()
        if k == 1:
            send[1, k, upper, :] = behind[:n].astype(BF)
            send[1, k, lower, :] = (behind[n:] + recv[1, 0, lower, :].astype(F32)).astype(BF)
        else:
            send[1, k] = (behind + recv[1, k - 1].astype(F32)).astype(BF)
        back_next.start()

    def rs_end(p, phase, block):
        own = block(z)
        go, back = rs_copies(p, phase, 3)
        go.wait_recv()
        back.wait_recv()
        recv = rs_recv.at[phase, p]
        return own + recv[0, 3].astype(F32) + recv[1, 3].astype(F32)

    def rs_drain(p, phase):
        for k in range(4):
            for copy in rs_copies(p, phase, k):
                copy.wait_send()

    def out_block(p):
        def block(f):
            lanes = pl.ds(pl.multiple_of(f * FB, FB), FB)
            return jnp.dot(
                attended[p * R : (p + 1) * R, :], wout[:, lanes], preferred_element_type=F32
            )

        return block

    def down_block(p):
        def block(f):
            lanes = pl.ds(pl.multiple_of(f * FB, FB), FB)
            return jnp.dot(
                hidden[p * R : (p + 1) * R, :], wdown[:, lanes], preferred_element_type=F32
            )

        return block

    def mix(p):
        rows = pl.ds(p * R, R)
        summed = rs_end(p, 0, out_block(p))
        mixed_all[p, z] = (own_stream[rows, :].astype(F32) + summed).astype(BF)

    def up_part(p, f, own=False):
        rows = pl.ds(p * R, R)
        wide = mixed_all[p, f].astype(F32)
        square = wide * wide
        square = square[:, :128] + square[:, 128:]
        lanes = pl.ds(pl.multiple_of(f * FB, FB), FB)
        normed = (wide * gain2_ref[:, lanes]).astype(BF)
        piece = jnp.dot(normed, wup[lanes, :], preferred_element_type=F32)
        if own:
            acc2[rows, :] = piece
            ssq2[rows, :] = square
        else:
            acc2[rows, :] += piece
            ssq2[rows, :] += square

    def activate(p):
        rows = pl.ds(p * R, R)
        total = jnp.sum(ssq2[rows, :], axis=1, keepdims=True)
        scale = lax.rsqrt(total * (1.0 / D) + 1e-6)
        hidden[rows, :] = jax.nn.gelu(acc2[rows, :] * scale, approximate=True).astype(BF)

    def last(p):
        rows = pl.ds(p * R, R)
        summed = rs_end(p, 1, down_block(p))
        out_ref[rows, :] = (mixed_all[p, z].astype(F32) + summed).astype(BF)

    def embed_work(g, k):
        embed_block(g, (z - 1 - k) & 7)
        if k < 3:
            embed_block(g, (z + 1 + k) & 7)

    def chain(p):
        give_wait(p)
        combine(p)
        for k in range(4):
            rs_step(p, 0, out_block(p), k)
            yield
        mix(p)
        ag_start(*mix_args[p], 0)
        up_part(p, z, own=True)
        yield
        for k in range(4):
            ag_wait(*mix_args[p], k)
            if k < 3:
                ag_start(*mix_args[p], k + 1)
            up_part(p, (z - 1 - k) & 7)
            if k < 3:
                up_part(p, (z + 1 + k) & 7)
                yield
        activate(p)
        for k in range(4):
            rs_step(p, 1, down_block(p), k)
            yield
        last(p)
        yield

    for k in range(4):
        ag_wait(*emb_args, k)
        if k < 3:
            ag_start(*emb_args, k + 1)
        for p in range(PARTS):
            ag_wait(*pos_args[p], k)
            if k < 3:
                ag_start(*pos_args[p], k + 1)
            if k > 0:
                embed_work(p, k - 1)
            if k == 3:
                embed_work(p, k)
                project(p)
                exchange_start(p)
        if k == 0:
            wait_cells()
            pool_inputs()
            weights[0].wait()
            for p in range(PARTS):
                embed_block(p, z, own=True)
    for i in range(1, 4):
        weights[i].wait()
    for p in range(PARTS):
        exchange_wait(p, True, True)
    attend()
    for p in range(PARTS):
        give_start(p)
    chains = [chain(p) for p in range(PARTS)]
    while chains:
        for each in list(chains):
            if next(each, 0) == 0:
                chains.remove(each)

    each_taker(lambda copy: copy.wait_send())
    ag_drain(*emb_args)
    for g in range(PARTS):
        exchange_drain(g)
    for p in range(PARTS):
        ag_drain(*pos_args[p])
        give_drain(p)
        rs_drain(p, 0)
        ag_drain(*mix_args[p])
        rs_drain(p, 1)


def body(latent, pos, embed, gain1, qkv_w, out_w, gain2, up, down):
    vmem = pl.BlockSpec(memory_space=pltpu.VMEM)
    hbm = pl.BlockSpec(memory_space=pl.ANY)
    dma = pltpu.SemaphoreType.DMA
    return pl.pallas_call(
        kernel,
        out_shape=jax.ShapeDtypeStruct((TOK, FB), BF),
        in_specs=[vmem, hbm, hbm, vmem, hbm, hbm, vmem, hbm, hbm],
        out_specs=vmem,
        scratch_shapes=[
            pltpu.VMEM((3, D, FB), BF),
            pltpu.VMEM((FB, D), BF),
            pltpu.VMEM((D, HID), BF),
            pltpu.VMEM((HID, D), BF),
            pltpu.VMEM((32, 64, 128), BF),
            pltpu.VMEM((NZ, TOK, FB), BF),
            pltpu.VMEM((NZ, C, FB), BF),
            pltpu.VMEM((TOK, 2048), BF),
            pltpu.VMEM((32, 128), F32),
            pltpu.VMEM((3, TOK, C), BF),
            pltpu.VMEM((TOK, FB), BF),
            pltpu.VMEM((TOK, 3 * FB), F32),
            pltpu.VMEM((TOK, 128), F32),
            pltpu.VMEM((2, TOK, 2 * HS), BF),
            pltpu.VMEM((2, TOK, HS), BF),
            pltpu.VMEM((KEYS, 2 * HS), BF),
            pltpu.VMEM((KEYS, HS), BF),
            pltpu.VMEM((PARTS, 8, MSG, HS), BF),
            pltpu.VMEM((PARTS, 8, MSG, HS), BF),
            pltpu.VMEM((TOK, 2 * HS), F32),
            pltpu.VMEM((TOK, 128), F32),
            pltpu.VMEM((TOK, FB), BF),
            pltpu.VMEM((2, PARTS, 2, 4, R, FB), BF),
            pltpu.VMEM((2, PARTS, 2, 4, R, FB), BF),
            pltpu.VMEM((PARTS, NZ, R, FB), BF),
            pltpu.VMEM((TOK, HID), F32),
            pltpu.VMEM((TOK, 128), F32),
            pltpu.VMEM((TOK, HID), BF),
            dma((6,)),
            dma((6,)),
            dma((32,)),
            dma((PARTS, 2, 4, 2)),
            dma((2, 4, 2)),
            dma((PARTS, 7)),
            dma((PARTS, 8)),
            dma((PARTS, 7)),
            dma((PARTS, 8)),
            dma((PARTS, 7)),
            dma((PARTS, 8)),
            dma((2, PARTS, 2, 4, 2)),
            dma((PARTS, 2, 4, 2)),
        ],
        compiler_params=pltpu.CompilerParams(
            collective_id=0, has_side_effects=True, vmem_limit_bytes=56 * 2**20
        ),
    )(
        latent,
        pos,
        embed,
        gain1.reshape(1, D),
        qkv_w,
        out_w,
        gain2.reshape(1, D),
        up,
        down,
    )


def solution(mesh):
    in_specs = (
        P("seq", None),
        P("seq", "head"),
        P(None, "head"),
        P(),
        P(None, None, "head"),
        P("head", None),
        P(),
        P(None, "head"),
        P("head", None),
    )
    return jax.shard_map(
        body, mesh=mesh, in_specs=in_specs, out_specs=P("seq", "head"), check_vma=False
    )
```

```python
import functools

import jax
import jax.numpy as jnp
from jax import lax
from jax.experimental import pallas as pl
from jax.experimental.pallas import tpu as pltpu
from jax.sharding import PartitionSpec as P

D = 2048
HS = 128
C = 32
TOK = 336
FB = 256
HID = 512
FIRST = 512
SECOND = 2560
PARTS = 3
R = TOK // PARTS
MSG = R + 16
NZ = 8
KEYS = 8 * TOK
NEG = -1e30
QSCALE = 1.4426950408889634 / HS**0.5
MESH = pl.DeviceIdType.MESH
BF = jnp.bfloat16
F32 = jnp.float32
NT = (((1,), (1,)), ((), ()))


def split3(wide):
    high = wide.astype(BF)
    rest = wide - high.astype(F32)
    mid = rest.astype(BF)
    low = (rest - mid.astype(F32)).astype(BF)
    return high, mid, low


def level(token):
    return (token >= FIRST).astype(jnp.int32) + (token >= SECOND).astype(jnp.int32)


def halves(rows, p):
    first = ((rows // 16 + p % 2) // 2) * 16
    return pl.ds(0, first), pl.ds(first, rows - first)


def kernel(
    latent_ref,
    pos_hbm,
    embed_hbm,
    gain1_ref,
    qkv_hbm,
    out_w_hbm,
    gain2_ref,
    up_hbm,
    down_hbm,
    out_ref,
    wqkv,
    wout,
    wup,
    wdown,
    grid_cells,
    pos_all,
    emb_all,
    select,
    lines_buf,
    inp,
    own_stream,
    acc,
    ssq,
    kv_send,
    q_send,
    kv_buf,
    q_buf,
    o_send,
    o_recv,
    state_o,
    state_m,
    attended,
    rs_send,
    rs_recv,
    mixed_all,
    acc2,
    ssq2,
    hidden,
    local_sem,
    cell_ssem,
    cell_rsem,
    pos_sem,
    emb_sem,
    kv_ssem,
    kv_rsem,
    q_ssem,
    q_rsem,
    o_ssem,
    o_rsem,
    rs_sem,
    mix_sem,
):
    seq = lax.axis_index("seq")
    z = lax.axis_index("head")
    x, y, c = seq >> 3, (seq >> 1) & 3, seq & 1
    right, left = (z + 1) & 7, (z + 7) & 7
    a0 = jnp.where(c == 0, x, y)
    b0 = jnp.where(c == 0, y, x)

    def sid(px, py, pc):
        return (px * 4 + py) * 2 + pc

    def ring(value, step):
        return (value + step) & 3

    sibling = sid(x, y, 1 - c)

    loads = [
        pltpu.make_async_copy(pos_hbm, pos_all.at[z], local_sem.at[0])
    ]
    loads.append(pltpu.make_async_copy(embed_hbm, emb_all.at[z], local_sem.at[1]))
    weights = [
        pltpu.make_async_copy(src, dst, local_sem.at[2 + i])
        for i, (src, dst) in enumerate(
            ((qkv_hbm, wqkv), (out_w_hbm, wout), (up_hbm, wup), (down_hbm, wdown))
        )
    ]
    for load in loads:
        load.start()
    for load in weights:
        load.start()

    wide = latent_ref[...].astype(F32)
    both = wide[0:1] + wide[1:2]
    for j in range(32):
        lines_buf[j : j + 1, :] = both[:, j * 128 : (j + 1) * 128]
    wide = lines_buf[...] * 0.25
    pooled = jnp.concatenate(
        [wide[:, 0:C] + wide[:, C : 2 * C], wide[:, 2 * C : 3 * C] + wide[:, 3 * C :]], axis=0
    )
    grid_cells[...] = jnp.zeros((32, 64, 128), BF)
    grid_cells[seq] = jnp.concatenate([*split3(pooled), jnp.zeros((64, C), BF)], axis=1)

    token = seq * TOK + lax.broadcasted_iota(jnp.int32, (TOK, 1), 0)
    top, mid_level = token >= SECOND, token >= FIRST
    from_top, from_mid = token - SECOND, token - FIRST
    key_top = (from_top >> 8) * 64 + ((from_top & 127) >> 1)
    key_mid = (from_mid >> 7) * 32 + ((from_mid & 63) >> 1)
    fine_key = jnp.where(top, key_top, -1)
    coarse_key = jnp.where(top, -1, jnp.where(mid_level, key_mid, token))
    col = lax.broadcasted_iota(jnp.int32, (1, 2048), 1)
    cell_row, cell_col = col >> 6, (col & 31) * 2 + ((col >> 5) & 1)
    fine_col = cell_row * 64 + cell_col
    coarse_col = (cell_row >> 1) * 32 + (cell_col >> 1)
    select[...] = jnp.where(
        fine_key == fine_col, 1.0, jnp.where(coarse_key == coarse_col, 0.25, 0.0)
    ).astype(BF)

    barrier = pltpu.get_barrier_semaphore()
    pl.semaphore_signal(barrier, inc=1, device_id={"head": right}, device_id_type=MESH)
    pl.semaphore_signal(barrier, inc=1, device_id={"head": left}, device_id_type=MESH)
    for step in range(1, 32):
        peer = (seq + step) & 31
        pl.semaphore_signal(barrier, inc=1, device_id={"seq": peer}, device_id_type=MESH)
    pl.semaphore_wait(barrier, 33)

    def remote(src, dst, ssem, rsem, **where):
        return pltpu.make_async_remote_copy(
            src_ref=src,
            dst_ref=dst,
            send_sem=ssem,
            recv_sem=rsem,
            device_id=where,
            device_id_type=MESH,
        )

    def ag_copies(buf, sems, base, rows, p, k):
        go, back = (z - k) & 7, (z + k) & 7
        if k == 3:
            upper, lower = halves(rows, p)
            upper = pl.ds(base + upper.start, upper.size)
            lower = pl.ds(base + lower.start, lower.size)
        else:
            upper = lower = pl.ds(base, rows)
        return (
            remote(buf.at[go, upper], buf.at[go, upper], sems.at[0, k, 0], sems.at[0, k, 1], head=right),
            remote(buf.at[back, lower], buf.at[back, lower], sems.at[1, k, 0], sems.at[1, k, 1], head=left),
        )

    def ag_start(*args):
        for copy in ag_copies(*args):
            copy.start()

    def ag_wait(*args):
        for copy in ag_copies(*args):
            copy.wait_recv()

    def ag_drain(*args):
        for k in range(4):
            for copy in ag_copies(*args, k):
                copy.wait_send()

    pos_args = [(pos_all, pos_sem.at[p], p * R, R, p) for p in range(PARTS)]
    emb_args = (emb_all, emb_sem, 0, C, 0)
    mix_args = [(mixed_all.at[p], mix_sem.at[p], 0, R, p) for p in range(PARTS)]

    for load in loads:
        load.wait()
    ag_start(*emb_args, 0)
    for p in range(PARTS):
        ag_start(*pos_args[p], 0)

    def takers(row):
        fine, coarse = SECOND + 256 * row, row >> 1
        middle, low = FIRST + 128 * coarse, 32 * coarse
        return (fine, fine + 255), (middle, middle + 127), (low, low + 31)

    def owner(token):
        return (token * 49933) >> 24

    def cell_copy(i, row, dest):
        return remote(
            grid_cells.at[row], grid_cells.at[row], cell_ssem.at[i], cell_rsem.at[row], seq=dest
        )

    def each_taker(act):
        for i, ends in enumerate(takers(seq)):
            one, two = owner(ends[0]), owner(ends[1])

            @pl.when(one != seq)
            def _():
                act(cell_copy(2 * i, seq, one))

            @pl.when(jnp.logical_and(two != one, two != seq))
            def _():
                act(cell_copy(2 * i + 1, seq, two))

    each_taker(lambda copy: copy.start())

    def wait_cells():
        start, end = seq * TOK, seq * TOK + TOK - 1

        def wait_rows(low, high):
            @pl.loop(low, high)
            def _(row):
                @pl.when(row != seq)
                def _():
                    cell_copy(0, row, sibling).wait_recv()

        @pl.when(end >= SECOND)
        def _():
            wait_rows(jnp.maximum(start - SECOND, 0) >> 8, ((end - SECOND) >> 8) + 1)

        @pl.when(jnp.logical_and(end >= FIRST, start < SECOND))
        def _():
            wait_rows(
                (jnp.maximum(start - FIRST, 0) >> 7) * 2,
                ((jnp.minimum(end, SECOND - 1) - FIRST) >> 7) * 2 + 2,
            )

        @pl.when(start < FIRST)
        def _():
            wait_rows((start >> 5) * 2, (jnp.minimum(end, FIRST - 1) >> 5) * 2 + 2)

    def pool_inputs():
        pooled = jnp.dot(
            select[...], grid_cells[...].reshape(2048, 128), preferred_element_type=F32
        )
        inputs = pooled[:, 0:C] + pooled[:, C : 2 * C] + pooled[:, 2 * C : 3 * C]
        for i, piece in enumerate(split3(inputs)):
            inp[i] = piece

    def group_rows(p):
        return pl.ds(p * R, R)

    def embed_block(g, f, own=False):
        rows = group_rows(g)
        emb = emb_all[f]
        wide = pos_all[f, rows, :].astype(F32)
        for i in range(3):
            wide = wide + jnp.dot(inp[i, rows, :], emb, preferred_element_type=F32)
        stream = wide.astype(BF)
        if own:
            own_stream[rows, :] = stream
        wide = stream.astype(F32)
        square = wide * wide
        square = square[:, :128] + square[:, 128:]
        lanes = pl.ds(pl.multiple_of(f * FB, FB), FB)
        normed = (wide * gain1_ref[:, lanes]).astype(BF)
        for j in range(3):
            piece = jnp.dot(normed, wqkv[j, lanes, :], preferred_element_type=F32)
            if own:
                acc[rows, j * FB : (j + 1) * FB] = piece
            else:
                acc[rows, j * FB : (j + 1) * FB] += piece
        if own:
            ssq[rows, :] = square
        else:
            ssq[rows, :] += square

    def project(g):
        rows = group_rows(g)
        total = jnp.sum(ssq[rows, :], axis=1, keepdims=True)
        scale = lax.rsqrt(total * (1.0 / D) + 1e-6)
        for h in range(2):
            cols = slice(h * HS, (h + 1) * HS)
            q_send[h, rows, :] = (acc[rows, cols] * (scale * QSCALE)).astype(BF)
            kv_send[h, rows, 0:HS] = (acc[rows, FB + h * HS : FB + (h + 1) * HS] * scale).astype(BF)
            kv_send[h, rows, HS:] = (
                acc[rows, 2 * FB + h * HS : 2 * FB + (h + 1) * HS] * scale
            ).astype(BF)

    def slot_rows(slot, g):
        return pl.ds(pl.multiple_of(slot * TOK + g * R, 16), R)

    def exchange(p):
        rows = group_rows(p)
        kv_copies, q_copies = [], []

        def kv_copy(i, head, slot, dest):
            return remote(
                kv_send.at[head, rows],
                kv_buf.at[slot_rows(slot, p)],
                kv_ssem.at[p, i],
                kv_rsem.at[p, slot],
                seq=dest,
            )

        def q_copy(i, head, slot, dest):
            return remote(
                q_send.at[head, rows],
                q_buf.at[slot_rows(slot, p)],
                q_ssem.at[p, i],
                q_rsem.at[p, slot],
                seq=dest,
            )

        other = 1 - c
        kv_copies.append(kv_copy(6, other, jnp.where(c == 1, x, y) * 2 + c, sibling))
        q_copies.append(q_copy(6, other, jnp.where(c == 1, y, x) * 2 + c, sibling))
        for i, step in enumerate((1, 3, 2)):
            kv_copies.append(kv_copy(i, 0, x * 2 + c, sid(ring(x, step), y, 0)))
            kv_copies.append(kv_copy(3 + i, 1, y * 2 + c, sid(x, ring(y, step), 1)))
            q_copies.append(q_copy(i, 0, y * 2 + c, sid(x, ring(y, step), 0)))
            q_copies.append(q_copy(3 + i, 1, x * 2 + c, sid(ring(x, step), y, 1)))
        return kv_copies, q_copies

    def exchange_start(p):
        rows = group_rows(p)
        kv_copies, q_copies = exchange(p)
        for copy in q_copies + kv_copies:
            copy.start()
        kv_buf[slot_rows(a0 * 2 + c, p), :] = kv_send[c, rows, :]
        q_buf[slot_rows(b0 * 2 + c, p), :] = q_send[c, rows, :]

    def exchange_wait(p, want_q, want_kv):
        rows = group_rows(p)
        for i in range(1, 8):
            if want_q:
                slot = (b0 * 2 + c + i) & 7
                remote(
                    q_send.at[0, rows],
                    q_buf.at[slot_rows(slot, p)],
                    q_ssem.at[p, 0],
                    q_rsem.at[p, slot],
                    seq=sibling,
                ).wait_recv()
            if want_kv:
                slot = (a0 * 2 + c + i) & 7
                remote(
                    kv_send.at[0, rows],
                    kv_buf.at[slot_rows(slot, p)],
                    kv_ssem.at[p, 0],
                    kv_rsem.at[p, slot],
                    seq=sibling,
                ).wait_recv()

    def exchange_drain(p):
        kv_copies, q_copies = exchange(p)
        for copy in q_copies + kv_copies:
            copy.wait_send()

    ones_row = jnp.ones((1, HS), BF)

    def values_and_ones(kv):
        return jnp.concatenate([kv[:, HS:], jnp.broadcast_to(ones_row, (kv.shape[0], HS))], axis=1)

    diag = lax.broadcasted_iota(jnp.int32, (128, 128), 0) == lax.broadcasted_iota(
        jnp.int32, (128, 128), 1
    )

    def finish(slot, total, largest):
        sums = total[:, HS:]
        normal = (total[:, :HS] / sums).astype(BF)
        log_sum = largest + jnp.log2(sums)
        for p in range(PARTS):
            low = p * R
            o_send[p, slot, 0:R, :] = normal[low : low + R]
            tile = jnp.concatenate(
                [log_sum[low : low + R], jnp.zeros((128 - R, 128), F32)], axis=0
            )
            line = jnp.sum(jnp.where(diag, tile, 0.0), axis=0, keepdims=True)
            packed = [v.astype(F32) for v in split3(line)] + [jnp.zeros((13, 128), F32)]
            o_send[p, slot, R:MSG, :] = jnp.concatenate(packed, axis=0).astype(BF)

    CHUNK = 896

    def plain_slot(slot):
        queries = q_buf[pl.ds(pl.multiple_of(slot * TOK, 16), TOK), :]
        largest = total = None
        for low in range(0, KEYS, CHUNK):
            kv = kv_buf[low : low + CHUNK, :]
            scores = lax.dot_general(queries, kv[:, :HS], NT, preferred_element_type=F32)
            newest = jnp.max(scores, axis=1, keepdims=True)
            if total is not None:
                newest = jnp.maximum(newest, largest)
            weights = jnp.exp2(scores - newest).astype(BF)
            part = jnp.dot(weights, values_and_ones(kv), preferred_element_type=F32)
            total = part if total is None else total * jnp.exp2(largest - newest) + part
            largest = newest
        finish(slot, total, largest)

    def masked_block(b, chunks):
        first_q = jnp.where(c == 0, x * 8 + b * 2, b * 8 + y * 2)
        state_m[...] = jnp.full((2, TOK, 128), NEG, F32)
        state_o[...] = jnp.zeros((2, TOK, 2 * HS), F32)

        @pl.loop(0, chunks)
        def _(i):
            low = pl.multiple_of(i * CHUNK, 128)
            kv = kv_buf[pl.ds(low, CHUNK), :]
            key = low + lax.broadcasted_iota(jnp.int32, (1, CHUNK), 1)
            block = sum((key >= edge * 2 * TOK).astype(jnp.int32) for edge in (1, 2, 3))
            shift = jnp.where(c == 0, block * (6 * TOK) + y * 2 * TOK, x * 8 * TOK)
            k_level = level(key + shift)
            for core in range(2):
                row = pl.multiple_of((b * 2 + core) * TOK, 16)
                queries = q_buf[pl.ds(row, TOK), :]
                scores = lax.dot_general(queries, kv[:, :HS], NT, preferred_element_type=F32)
                token = (first_q + core) * TOK + lax.broadcasted_iota(jnp.int32, (TOK, 1), 0)
                scores = jnp.where(k_level <= level(token), scores, NEG)
                before = state_m[core, :, 0:1]
                newest = jnp.maximum(before, jnp.max(scores, axis=1, keepdims=True))
                weights = jnp.exp2(scores - newest).astype(BF)
                part = jnp.dot(weights, values_and_ones(kv), preferred_element_type=F32)
                state_o[core] = state_o[core] * jnp.exp2(before - newest) + part
                state_m[core] = jnp.broadcast_to(newest, (TOK, 128))

        @pl.loop(0, 2)
        def _(core):
            finish(b * 2 + core, state_o[core], state_m[core, :, 0:1])

    def give_copies(slot, act, keep):
        b, core = slot >> 1, slot & 1
        dest = jnp.where(c == 0, sid(x, b, core), sid(b, y, core))

        @pl.when(dest != seq)
        def _():
            for p in range(PARTS):
                act(
                    remote(
                        o_send.at[p, slot],
                        o_recv.at[p, c * 4 + b0],
                        o_ssem.at[p, slot],
                        o_rsem.at[p, c * 4 + b0],
                        seq=dest,
                    )
                )

        if keep:

            @pl.when(dest == seq)
            def _():
                for p in range(PARTS):
                    o_recv[p, c * 4 + b0] = o_send[p, slot]

    def give_block(b):
        @pl.loop(0, 2)
        def _(core):
            give_copies(b * 2 + core, lambda copy: copy.start(), True)

    def give_drain():
        @pl.loop(0, 8)
        def _(slot):
            give_copies(slot, lambda copy: copy.wait_send(), False)

    def attend():
        first_plain = jnp.where(c == 0, jnp.where(x == 0, 4, 0), 1)
        nothing = jnp.logical_and(c == 1, jnp.logical_and(x >= 1, y < 3))

        @pl.when(nothing)
        def _():
            for i in range(2):
                for p in range(PARTS):
                    o_send[p, i, 0:R, :] = jnp.zeros((R, HS), BF)
                    o_send[p, i, R:MSG, :] = jnp.full((MSG - R, HS), NEG, BF)
            give_block(0)

        @pl.when(jnp.logical_not(nothing))
        def _():
            @pl.loop(0, first_plain)
            def _(b):
                masked_block(b, jnp.where(jnp.logical_and(c == 0, b < 3), 1, 3))
                give_block(b)

        @pl.loop(first_plain, 4)
        def _(i):
            turn = b0 + i - first_plain
            turn = jnp.where(turn >= 3, turn - 3, turn)
            b = jnp.where(c == 0, (b0 + 1 + i) & 3, 1 + turn)
            plain_slot(b * 2)
            plain_slot(b * 2 + 1)
            give_block(b)

    def give_wait(p):
        for i in range(1, 8):
            slot = (c * 4 + b0 + i) & 7
            remote(
                o_send.at[p, 0],
                o_recv.at[p, slot],
                o_ssem.at[p, 0],
                o_rsem.at[p, slot],
                seq=sibling,
            ).wait_recv()

    def combine(p):
        tails = [o_recv[p, i, R:MSG, :].astype(F32) for i in range(8)]
        logs = [t[0:1] + t[1:2] + t[2:3] for t in tails]
        for h in range(2):
            four = logs[h * 4 : h * 4 + 4]
            largest = functools.reduce(jnp.maximum, four)
            powers = [jnp.exp2(v - largest) for v in four]
            total = powers[0] + powers[1] + powers[2] + powers[3]
            mean = None
            for a in range(4):
                share = jnp.sum(
                    jnp.where(diag, powers[a] / total, 0.0), axis=1, keepdims=True
                )
                term = o_recv[p, h * 4 + a, 0:R, :].astype(F32) * share[:R]
                mean = term if mean is None else mean + term
            attended[p * R : (p + 1) * R, h * HS : (h + 1) * HS] = mean.astype(BF)

    def rs_copies(p, phase, k):
        upper, lower = halves(R, p)
        if k > 0:
            upper = lower = pl.ds(0, R)
        send, recv, sems = rs_send.at[phase, p], rs_recv.at[phase, p], rs_sem.at[phase, p]
        return (
            remote(send.at[0, k, upper], recv.at[0, k, upper], sems.at[0, k, 0], sems.at[0, k, 1], head=right),
            remote(send.at[1, k, lower], recv.at[1, k, lower], sems.at[1, k, 0], sems.at[1, k, 1], head=left),
        )

    def rs_step(p, phase, block, k):
        upper, lower = halves(R, p)
        send, recv = rs_send.at[phase, p], rs_recv.at[phase, p]
        if k == 0:
            term = block((z + 4) & 7).astype(BF)
            send[0, 0, upper, :] = term[upper.start : upper.start + upper.size]
            send[1, 0, lower, :] = term[lower.start : lower.start + lower.size]
            for copy in rs_copies(p, phase, 0):
                copy.start()
            return
        ahead = block((z + 4 - k) & 7)
        behind = block((z + 4 + k) & 7)
        go, back = rs_copies(p, phase, k - 1)
        go_next, back_next = rs_copies(p, phase, k)
        go.wait_recv()
        if k == 1:
            n = upper.size
            send[0, k, upper, :] = (ahead[:n] + recv[0, 0, upper, :].astype(F32)).astype(BF)
            send[0, k, lower, :] = ahead[n:].astype(BF)
        else:
            send[0, k] = (ahead + recv[0, k - 1].astype(F32)).astype(BF)
        go_next.start()
        back.wait_recv()
        if k == 1:
            send[1, k, upper, :] = behind[:n].astype(BF)
            send[1, k, lower, :] = (behind[n:] + recv[1, 0, lower, :].astype(F32)).astype(BF)
        else:
            send[1, k] = (behind + recv[1, k - 1].astype(F32)).astype(BF)
        back_next.start()

    def rs_end(p, phase, block):
        own = block(z)
        go, back = rs_copies(p, phase, 3)
        go.wait_recv()
        back.wait_recv()
        recv = rs_recv.at[phase, p]
        return own + recv[0, 3].astype(F32) + recv[1, 3].astype(F32)

    def rs_drain(p, phase):
        for k in range(4):
            for copy in rs_copies(p, phase, k):
                copy.wait_send()

    def out_block(p):
        def block(f):
            lanes = pl.ds(pl.multiple_of(f * FB, FB), FB)
            return jnp.dot(
                attended[p * R : (p + 1) * R, :], wout[:, lanes], preferred_element_type=F32
            )

        return block

    def down_block(p):
        def block(f):
            lanes = pl.ds(pl.multiple_of(f * FB, FB), FB)
            return jnp.dot(
                hidden[p * R : (p + 1) * R, :], wdown[:, lanes], preferred_element_type=F32
            )

        return block

    def mix(p):
        rows = pl.ds(p * R, R)
        summed = rs_end(p, 0, out_block(p))
        mixed_all[p, z] = (own_stream[rows, :].astype(F32) + summed).astype(BF)

    def up_part(p, f, own=False):
        rows = pl.ds(p * R, R)
        wide = mixed_all[p, f].astype(F32)
        square = wide * wide
        square = square[:, :128] + square[:, 128:]
        lanes = pl.ds(pl.multiple_of(f * FB, FB), FB)
        normed = (wide * gain2_ref[:, lanes]).astype(BF)
        piece = jnp.dot(normed, wup[lanes, :], preferred_element_type=F32)
        if own:
            acc2[rows, :] = piece
            ssq2[rows, :] = square
        else:
            acc2[rows, :] += piece
            ssq2[rows, :] += square

    def activate(p):
        rows = pl.ds(p * R, R)
        total = jnp.sum(ssq2[rows, :], axis=1, keepdims=True)
        scale = lax.rsqrt(total * (1.0 / D) + 1e-6)
        hidden[rows, :] = jax.nn.gelu(acc2[rows, :] * scale, approximate=True).astype(BF)

    def last(p):
        rows = pl.ds(p * R, R)
        summed = rs_end(p, 1, down_block(p))
        out_ref[rows, :] = (mixed_all[p, z].astype(F32) + summed).astype(BF)

    def embed_work(g, k):
        embed_block(g, (z - 1 - k) & 7)
        if k < 3:
            embed_block(g, (z + 1 + k) & 7)

    def chain(p):
        give_wait(p)
        combine(p)
        for k in range(4):
            rs_step(p, 0, out_block(p), k)
            yield
        mix(p)
        ag_start(*mix_args[p], 0)
        up_part(p, z, own=True)
        yield
        for k in range(4):
            ag_wait(*mix_args[p], k)
            if k < 3:
                ag_start(*mix_args[p], k + 1)
            up_part(p, (z - 1 - k) & 7)
            if k < 3:
                up_part(p, (z + 1 + k) & 7)
                yield
        activate(p)
        for k in range(4):
            rs_step(p, 1, down_block(p), k)
            yield
        last(p)
        yield

    for k in range(4):
        ag_wait(*emb_args, k)
        if k < 3:
            ag_start(*emb_args, k + 1)
        for p in range(PARTS):
            ag_wait(*pos_args[p], k)
            if k < 3:
                ag_start(*pos_args[p], k + 1)
            if k > 0:
                embed_work(p, k - 1)
            if k == 3:
                embed_work(p, k)
                project(p)
                exchange_start(p)
        if k == 0:
            wait_cells()
            pool_inputs()
            weights[0].wait()
            for p in range(PARTS):
                embed_block(p, z, own=True)
    for i in range(1, 4):
        weights[i].wait()
    for p in range(PARTS):
        exchange_wait(p, True, True)
    attend()
    chains = [chain(p) for p in range(PARTS)]
    while chains:
        for each in list(chains):
            if next(each, 0) == 0:
                chains.remove(each)

    each_taker(lambda copy: copy.wait_send())
    give_drain()
    ag_drain(*emb_args)
    for g in range(PARTS):
        exchange_drain(g)
    for p in range(PARTS):
        ag_drain(*pos_args[p])
        rs_drain(p, 0)
        ag_drain(*mix_args[p])
        rs_drain(p, 1)


def body(latent, pos, embed, gain1, qkv_w, out_w, gain2, up, down):
    vmem = pl.BlockSpec(memory_space=pltpu.VMEM)
    hbm = pl.BlockSpec(memory_space=pl.ANY)
    dma = pltpu.SemaphoreType.DMA
    return pl.pallas_call(
        kernel,
        out_shape=jax.ShapeDtypeStruct((TOK, FB), BF),
        in_specs=[vmem, hbm, hbm, vmem, hbm, hbm, vmem, hbm, hbm],
        out_specs=vmem,
        scratch_shapes=[
            pltpu.VMEM((3, D, FB), BF),
            pltpu.VMEM((FB, D), BF),
            pltpu.VMEM((D, HID), BF),
            pltpu.VMEM((HID, D), BF),
            pltpu.VMEM((32, 64, 128), BF),
            pltpu.VMEM((NZ, TOK, FB), BF),
            pltpu.VMEM((NZ, C, FB), BF),
            pltpu.VMEM((TOK, 2048), BF),
            pltpu.VMEM((32, 128), F32),
            pltpu.VMEM((3, TOK, C), BF),
            pltpu.VMEM((TOK, FB), BF),
            pltpu.VMEM((TOK, 3 * FB), F32),
            pltpu.VMEM((TOK, 128), F32),
            pltpu.VMEM((2, TOK, 2 * HS), BF),
            pltpu.VMEM((2, TOK, HS), BF),
            pltpu.VMEM((KEYS, 2 * HS), BF),
            pltpu.VMEM((KEYS, HS), BF),
            pltpu.VMEM((PARTS, 8, MSG, HS), BF),
            pltpu.VMEM((PARTS, 8, MSG, HS), BF),
            pltpu.VMEM((2, TOK, 2 * HS), F32),
            pltpu.VMEM((2, TOK, 128), F32),
            pltpu.VMEM((TOK, FB), BF),
            pltpu.VMEM((2, PARTS, 2, 4, R, FB), BF),
            pltpu.VMEM((2, PARTS, 2, 4, R, FB), BF),
            pltpu.VMEM((PARTS, NZ, R, FB), BF),
            pltpu.VMEM((TOK, HID), F32),
            pltpu.VMEM((TOK, 128), F32),
            pltpu.VMEM((TOK, HID), BF),
            dma((6,)),
            dma((6,)),
            dma((32,)),
            dma((PARTS, 2, 4, 2)),
            dma((2, 4, 2)),
            dma((PARTS, 7)),
            dma((PARTS, 8)),
            dma((PARTS, 7)),
            dma((PARTS, 8)),
            dma((PARTS, 8)),
            dma((PARTS, 8)),
            dma((2, PARTS, 2, 4, 2)),
            dma((PARTS, 2, 4, 2)),
        ],
        compiler_params=pltpu.CompilerParams(
            collective_id=0, has_side_effects=True, vmem_limit_bytes=56 * 2**20
        ),
    )(
        latent,
        pos,
        embed,
        gain1.reshape(1, D),
        qkv_w,
        out_w,
        gain2.reshape(1, D),
        up,
        down,
    )


def solution(mesh):
    in_specs = (
        P("seq", None),
        P("seq", "head"),
        P(None, "head"),
        P(),
        P(None, None, "head"),
        P("head", None),
        P(),
        P(None, "head"),
        P("head", None),
    )
    return jax.shard_map(
        body, mesh=mesh, in_specs=in_specs, out_specs=P("seq", "head"), check_vma=False
    )
```

```python
import functools

import jax
import jax.numpy as jnp
from jax import lax
from jax.experimental import pallas as pl
from jax.experimental.pallas import tpu as pltpu
from jax.sharding import PartitionSpec as P

D = 2048
HS = 128
C = 32
TOK = 336
FB = 256
HID = 512
FIRST = 512
SECOND = 2560
PARTS = 3
R = TOK // PARTS
MSG = R + 16
NZ = 8
KEYS = 8 * TOK
NEG = -1e30
QSCALE = 1.4426950408889634 / HS**0.5
MESH = pl.DeviceIdType.MESH
BF = jnp.bfloat16
F32 = jnp.float32
NT = (((1,), (1,)), ((), ()))


def split3(wide):
    high = wide.astype(BF)
    rest = wide - high.astype(F32)
    mid = rest.astype(BF)
    low = (rest - mid.astype(F32)).astype(BF)
    return high, mid, low


def level(token):
    return (token >= FIRST).astype(jnp.int32) + (token >= SECOND).astype(jnp.int32)


def halves(rows, p):
    first = ((rows // 16 + p % 2) // 2) * 16
    return pl.ds(0, first), pl.ds(first, rows - first)


def kernel(
    latent_ref,
    pos_hbm,
    embed_hbm,
    gain1_ref,
    qkv_hbm,
    out_w_hbm,
    gain2_ref,
    up_hbm,
    down_hbm,
    out_ref,
    wqkv,
    wout,
    wup,
    wdown,
    grid_cells,
    pos_all,
    emb_all,
    select,
    lines_buf,
    inp,
    own_stream,
    acc,
    ssq,
    kv_send,
    q_send,
    kv_buf,
    q_buf,
    o_send,
    o_recv,
    state_o,
    state_m,
    attended,
    rs_send,
    rs_recv,
    mixed_all,
    acc2,
    ssq2,
    hidden,
    local_sem,
    cell_ssem,
    cell_rsem,
    pos_sem,
    emb_sem,
    kv_ssem,
    kv_rsem,
    q_ssem,
    q_rsem,
    o_ssem,
    o_rsem,
    rs_sem,
    mix_sem,
):
    seq = lax.axis_index("seq")
    z = lax.axis_index("head")
    x, y, c = seq >> 3, (seq >> 1) & 3, seq & 1
    right, left = (z + 1) & 7, (z + 7) & 7
    a0 = jnp.where(c == 0, x, y)
    b0 = jnp.where(c == 0, y, x)

    def sid(px, py, pc):
        return (px * 4 + py) * 2 + pc

    def ring(value, step):
        return (value + step) & 3

    sibling = sid(x, y, 1 - c)

    loads = [
        pltpu.make_async_copy(pos_hbm, pos_all.at[z], local_sem.at[0])
    ]
    loads.append(pltpu.make_async_copy(embed_hbm, emb_all.at[z], local_sem.at[1]))
    weights = [
        pltpu.make_async_copy(src, dst, local_sem.at[2 + i])
        for i, (src, dst) in enumerate(
            ((qkv_hbm, wqkv), (out_w_hbm, wout), (up_hbm, wup), (down_hbm, wdown))
        )
    ]
    for load in loads:
        load.start()
    for load in weights:
        load.start()

    wide = latent_ref[...].astype(F32)
    both = wide[0:1] + wide[1:2]
    for j in range(32):
        lines_buf[j : j + 1, :] = both[:, j * 128 : (j + 1) * 128]
    wide = lines_buf[...] * 0.25
    pooled = jnp.concatenate(
        [wide[:, 0:C] + wide[:, C : 2 * C], wide[:, 2 * C : 3 * C] + wide[:, 3 * C :]], axis=0
    )
    grid_cells[...] = jnp.zeros((32, 64, 128), BF)
    grid_cells[seq] = jnp.concatenate([*split3(pooled), jnp.zeros((64, C), BF)], axis=1)

    token = seq * TOK + lax.broadcasted_iota(jnp.int32, (TOK, 1), 0)
    top, mid_level = token >= SECOND, token >= FIRST
    from_top, from_mid = token - SECOND, token - FIRST
    key_top = (from_top >> 8) * 64 + ((from_top & 127) >> 1)
    key_mid = (from_mid >> 7) * 32 + ((from_mid & 63) >> 1)
    fine_key = jnp.where(top, key_top, -1)
    coarse_key = jnp.where(top, -1, jnp.where(mid_level, key_mid, token))
    col = lax.broadcasted_iota(jnp.int32, (1, 2048), 1)
    cell_row, cell_col = col >> 6, (col & 31) * 2 + ((col >> 5) & 1)
    fine_col = cell_row * 64 + cell_col
    coarse_col = (cell_row >> 1) * 32 + (cell_col >> 1)
    select[...] = jnp.where(
        fine_key == fine_col, 1.0, jnp.where(coarse_key == coarse_col, 0.25, 0.0)
    ).astype(BF)

    barrier = pltpu.get_barrier_semaphore()
    pl.semaphore_signal(barrier, inc=1, device_id={"head": right}, device_id_type=MESH)
    pl.semaphore_signal(barrier, inc=1, device_id={"head": left}, device_id_type=MESH)
    for step in range(1, 32):
        peer = (seq + step) & 31
        pl.semaphore_signal(barrier, inc=1, device_id={"seq": peer}, device_id_type=MESH)
    pl.semaphore_wait(barrier, 33)

    def remote(src, dst, ssem, rsem, **where):
        return pltpu.make_async_remote_copy(
            src_ref=src,
            dst_ref=dst,
            send_sem=ssem,
            recv_sem=rsem,
            device_id=where,
            device_id_type=MESH,
        )

    def ag_copies(buf, sems, base, rows, p, k):
        go, back = (z - k) & 7, (z + k) & 7
        if k == 3:
            upper, lower = halves(rows, p)
            upper = pl.ds(base + upper.start, upper.size)
            lower = pl.ds(base + lower.start, lower.size)
        else:
            upper = lower = pl.ds(base, rows)
        return (
            remote(buf.at[go, upper], buf.at[go, upper], sems.at[0, k, 0], sems.at[0, k, 1], head=right),
            remote(buf.at[back, lower], buf.at[back, lower], sems.at[1, k, 0], sems.at[1, k, 1], head=left),
        )

    def ag_start(*args):
        for copy in ag_copies(*args):
            copy.start()

    def ag_step(*args):
        *where, k = args
        here = ag_copies(*where, k)
        if k == 3:
            for copy in here:
                copy.wait_recv()
            return
        for copy, onward in zip(here, ag_copies(*where, k + 1)):
            copy.wait_recv()
            onward.start()

    def ag_drain(*args):
        for k in range(4):
            for copy in ag_copies(*args, k):
                copy.wait_send()

    pos_args = [(pos_all, pos_sem.at[p], p * R, R, p) for p in range(PARTS)]
    emb_args = (emb_all, emb_sem, 0, C, 0)
    mix_args = [(mixed_all.at[p], mix_sem.at[p], 0, R, p) for p in range(PARTS)]

    for load in loads:
        load.wait()
    ag_start(*emb_args, 0)
    for p in range(PARTS):
        ag_start(*pos_args[p], 0)

    def takers(row):
        fine, coarse = SECOND + 256 * row, row >> 1
        middle, low = FIRST + 128 * coarse, 32 * coarse
        return (fine, fine + 255), (middle, middle + 127), (low, low + 31)

    def owner(token):
        return (token * 49933) >> 24

    def cell_copy(i, row, dest):
        return remote(
            grid_cells.at[row], grid_cells.at[row], cell_ssem.at[i], cell_rsem.at[row], seq=dest
        )

    def each_taker(act):
        for i, ends in enumerate(takers(seq)):
            one, two = owner(ends[0]), owner(ends[1])

            @pl.when(one != seq)
            def _():
                act(cell_copy(2 * i, seq, one))

            @pl.when(jnp.logical_and(two != one, two != seq))
            def _():
                act(cell_copy(2 * i + 1, seq, two))

    each_taker(lambda copy: copy.start())

    def wait_cells():
        start, end = seq * TOK, seq * TOK + TOK - 1

        def wait_rows(low, high):
            @pl.loop(low, high)
            def _(row):
                @pl.when(row != seq)
                def _():
                    cell_copy(0, row, sibling).wait_recv()

        @pl.when(end >= SECOND)
        def _():
            wait_rows(jnp.maximum(start - SECOND, 0) >> 8, ((end - SECOND) >> 8) + 1)

        @pl.when(jnp.logical_and(end >= FIRST, start < SECOND))
        def _():
            wait_rows(
                (jnp.maximum(start - FIRST, 0) >> 7) * 2,
                ((jnp.minimum(end, SECOND - 1) - FIRST) >> 7) * 2 + 2,
            )

        @pl.when(start < FIRST)
        def _():
            wait_rows((start >> 5) * 2, (jnp.minimum(end, FIRST - 1) >> 5) * 2 + 2)

    def pool_inputs():
        pooled = jnp.dot(
            select[...], grid_cells[...].reshape(2048, 128), preferred_element_type=F32
        )
        inputs = pooled[:, 0:C] + pooled[:, C : 2 * C] + pooled[:, 2 * C : 3 * C]
        for i, piece in enumerate(split3(inputs)):
            inp[i] = piece

    def group_rows(p):
        return pl.ds(p * R, R)

    def embed_block(g, f, own=False):
        rows = group_rows(g)
        emb = emb_all[f]
        wide = pos_all[f, rows, :].astype(F32)
        for i in range(3):
            wide = wide + jnp.dot(inp[i, rows, :], emb, preferred_element_type=F32)
        stream = wide.astype(BF)
        if own:
            own_stream[rows, :] = stream
        wide = stream.astype(F32)
        square = wide * wide
        square = square[:, :128] + square[:, 128:]
        lanes = pl.ds(pl.multiple_of(f * FB, FB), FB)
        normed = (wide * gain1_ref[:, lanes]).astype(BF)
        for j in range(3):
            piece = jnp.dot(normed, wqkv[j, lanes, :], preferred_element_type=F32)
            if own:
                acc[rows, j * FB : (j + 1) * FB] = piece
            else:
                acc[rows, j * FB : (j + 1) * FB] += piece
        if own:
            ssq[rows, :] = square
        else:
            ssq[rows, :] += square

    def project(g):
        rows = group_rows(g)
        total = jnp.sum(ssq[rows, :], axis=1, keepdims=True)
        scale = lax.rsqrt(total * (1.0 / D) + 1e-6)
        for h in range(2):
            cols = slice(h * HS, (h + 1) * HS)
            q_send[h, rows, :] = (acc[rows, cols] * (scale * QSCALE)).astype(BF)
            kv_send[h, rows, 0:HS] = (acc[rows, FB + h * HS : FB + (h + 1) * HS] * scale).astype(BF)
            kv_send[h, rows, HS:] = (
                acc[rows, 2 * FB + h * HS : 2 * FB + (h + 1) * HS] * scale
            ).astype(BF)

    def slot_rows(slot, g):
        return pl.ds(pl.multiple_of(slot * TOK + g * R, 16), R)

    def exchange(p):
        rows = group_rows(p)
        kv_copies, q_copies = [], []

        def kv_copy(i, head, slot, dest):
            return remote(
                kv_send.at[head, rows],
                kv_buf.at[slot_rows(slot, p)],
                kv_ssem.at[p, i],
                kv_rsem.at[p, slot],
                seq=dest,
            )

        def q_copy(i, head, slot, dest):
            return remote(
                q_send.at[head, rows],
                q_buf.at[slot_rows(slot, p)],
                q_ssem.at[p, i],
                q_rsem.at[p, slot],
                seq=dest,
            )

        other = 1 - c
        kv_copies.append(kv_copy(6, other, jnp.where(c == 1, x, y) * 2 + c, sibling))
        q_copies.append(q_copy(6, other, jnp.where(c == 1, y, x) * 2 + c, sibling))
        for i, step in enumerate((3, 2, 1)):
            kv_copies.append(kv_copy(i, 0, x * 2 + c, sid(ring(x, step), y, 0)))
            kv_copies.append(kv_copy(3 + i, 1, y * 2 + c, sid(x, ring(y, step), 1)))
            q_copies.append(q_copy(i, 0, y * 2 + c, sid(x, ring(y, step), 0)))
            q_copies.append(q_copy(3 + i, 1, x * 2 + c, sid(ring(x, step), y, 1)))
        return kv_copies, q_copies

    def exchange_start(p):
        rows = group_rows(p)
        for copy in exchange(p)[0]:
            copy.start()
        kv_buf[slot_rows(a0 * 2 + c, p), :] = kv_send[c, rows, :]
        q_buf[slot_rows(b0 * 2 + c, p), :] = q_send[c, rows, :]

    def queries_start():
        copies = [exchange(p)[1] for p in range(PARTS)]
        for i in (1, 2, 3, 4, 5, 6, 0):
            for p in range(PARTS):
                copies[p][i].start()

    def queries_wait(b):
        @pl.loop(0, 2)
        def _(core):
            slot = b * 2 + core

            @pl.when(slot != b0 * 2 + c)
            def _():
                for p in range(PARTS):
                    remote(
                        q_send.at[0, group_rows(p)],
                        q_buf.at[slot_rows(slot, p)],
                        q_ssem.at[p, 0],
                        q_rsem.at[p, slot],
                        seq=sibling,
                    ).wait_recv()

    def exchange_wait(p):
        rows = group_rows(p)
        for i in range(1, 8):
            slot = (a0 * 2 + c + i) & 7
            remote(
                kv_send.at[0, rows],
                kv_buf.at[slot_rows(slot, p)],
                kv_ssem.at[p, 0],
                kv_rsem.at[p, slot],
                seq=sibling,
            ).wait_recv()

    def exchange_drain(p):
        kv_copies, q_copies = exchange(p)
        for copy in q_copies + kv_copies:
            copy.wait_send()

    ones_row = jnp.ones((1, HS), BF)

    def values_and_ones(kv):
        return jnp.concatenate([kv[:, HS:], jnp.broadcast_to(ones_row, (kv.shape[0], HS))], axis=1)

    diag = lax.broadcasted_iota(jnp.int32, (128, 128), 0) == lax.broadcasted_iota(
        jnp.int32, (128, 128), 1
    )

    def finish(slot, total, largest):
        sums = total[:, HS:]
        normal = (total[:, :HS] / sums).astype(BF)
        log_sum = largest + jnp.log2(sums)
        for p in range(PARTS):
            low = p * R
            o_send[p, slot, 0:R, :] = normal[low : low + R]
            tile = jnp.concatenate(
                [log_sum[low : low + R], jnp.zeros((128 - R, 128), F32)], axis=0
            )
            line = jnp.sum(jnp.where(diag, tile, 0.0), axis=0, keepdims=True)
            packed = [v.astype(F32) for v in split3(line)] + [jnp.zeros((13, 128), F32)]
            o_send[p, slot, R:MSG, :] = jnp.concatenate(packed, axis=0).astype(BF)

    CHUNK = 896

    def plain_slot(slot):
        queries = q_buf[pl.ds(pl.multiple_of(slot * TOK, 16), TOK), :]
        largest = total = None
        for low in range(0, KEYS, CHUNK):
            kv = kv_buf[low : low + CHUNK, :]
            scores = lax.dot_general(queries, kv[:, :HS], NT, preferred_element_type=F32)
            newest = jnp.max(scores, axis=1, keepdims=True)
            if total is not None:
                newest = jnp.maximum(newest, largest)
            weights = jnp.exp2(scores - newest).astype(BF)
            part = jnp.dot(weights, values_and_ones(kv), preferred_element_type=F32)
            total = part if total is None else total * jnp.exp2(largest - newest) + part
            largest = newest
        finish(slot, total, largest)

    def masked_block(b, chunks):
        first_q = jnp.where(c == 0, x * 8 + b * 2, b * 8 + y * 2)
        state_m[...] = jnp.full((2, TOK, 128), NEG, F32)
        state_o[...] = jnp.zeros((2, TOK, 2 * HS), F32)

        @pl.loop(0, chunks)
        def _(i):
            low = pl.multiple_of(i * CHUNK, 128)
            kv = kv_buf[pl.ds(low, CHUNK), :]
            key = low + lax.broadcasted_iota(jnp.int32, (1, CHUNK), 1)
            block = sum((key >= edge * 2 * TOK).astype(jnp.int32) for edge in (1, 2, 3))
            shift = jnp.where(c == 0, block * (6 * TOK) + y * 2 * TOK, x * 8 * TOK)
            k_level = level(key + shift)
            for core in range(2):
                row = pl.multiple_of((b * 2 + core) * TOK, 16)
                queries = q_buf[pl.ds(row, TOK), :]
                scores = lax.dot_general(queries, kv[:, :HS], NT, preferred_element_type=F32)
                token = (first_q + core) * TOK + lax.broadcasted_iota(jnp.int32, (TOK, 1), 0)
                scores = jnp.where(k_level <= level(token), scores, NEG)
                before = state_m[core, :, 0:1]
                newest = jnp.maximum(before, jnp.max(scores, axis=1, keepdims=True))
                weights = jnp.exp2(scores - newest).astype(BF)
                part = jnp.dot(weights, values_and_ones(kv), preferred_element_type=F32)
                state_o[core] = state_o[core] * jnp.exp2(before - newest) + part
                state_m[core] = jnp.broadcast_to(newest, (TOK, 128))

        @pl.loop(0, 2)
        def _(core):
            finish(b * 2 + core, state_o[core], state_m[core, :, 0:1])

    def give_copies(slot, act, keep):
        b, core = slot >> 1, slot & 1
        dest = jnp.where(c == 0, sid(x, b, core), sid(b, y, core))

        @pl.when(dest != seq)
        def _():
            for p in range(PARTS):
                act(
                    remote(
                        o_send.at[p, slot],
                        o_recv.at[p, c * 4 + b0],
                        o_ssem.at[p, slot],
                        o_rsem.at[p, c * 4 + b0],
                        seq=dest,
                    )
                )

        if keep:

            @pl.when(dest == seq)
            def _():
                for p in range(PARTS):
                    o_recv[p, c * 4 + b0] = o_send[p, slot]

    def give_block(b):
        @pl.loop(0, 2)
        def _(core):
            give_copies(b * 2 + core, lambda copy: copy.start(), True)

    def give_drain():
        @pl.loop(0, 8)
        def _(slot):
            give_copies(slot, lambda copy: copy.wait_send(), False)

    def attend():
        first_plain = jnp.where(c == 0, jnp.where(x == 0, 4, 0), 1)
        nothing = jnp.logical_and(c == 1, jnp.logical_and(x >= 1, y < 3))

        @pl.when(nothing)
        def _():
            for i in range(2):
                for p in range(PARTS):
                    o_send[p, i, 0:R, :] = jnp.zeros((R, HS), BF)
                    o_send[p, i, R:MSG, :] = jnp.full((MSG - R, HS), NEG, BF)
            give_block(0)

        @pl.when(jnp.logical_not(nothing))
        def _():
            @pl.loop(0, first_plain)
            def _(b):
                queries_wait(b)
                masked_block(b, jnp.where(jnp.logical_and(c == 0, b < 3), 1, 3))
                give_block(b)

        @pl.loop(first_plain, 4)
        def _(i):
            turn = b0 + i - first_plain
            turn = jnp.where(turn >= 3, turn - 3, turn)
            b = jnp.where(c == 0, (b0 + 1 + i) & 3, 1 + turn)
            queries_wait(b)
            plain_slot(b * 2)
            plain_slot(b * 2 + 1)
            give_block(b)

        @pl.when(nothing)
        def _():
            queries_wait(0)

    def give_wait(p):
        for i in range(1, 8):
            slot = (c * 4 + b0 + i) & 7
            remote(
                o_send.at[p, 0],
                o_recv.at[p, slot],
                o_ssem.at[p, 0],
                o_rsem.at[p, slot],
                seq=sibling,
            ).wait_recv()

    def combine(p):
        tails = [o_recv[p, i, R:MSG, :].astype(F32) for i in range(8)]
        logs = [t[0:1] + t[1:2] + t[2:3] for t in tails]
        for h in range(2):
            four = logs[h * 4 : h * 4 + 4]
            largest = functools.reduce(jnp.maximum, four)
            powers = [jnp.exp2(v - largest) for v in four]
            total = powers[0] + powers[1] + powers[2] + powers[3]
            mean = None
            for a in range(4):
                share = jnp.sum(
                    jnp.where(diag, powers[a] / total, 0.0), axis=1, keepdims=True
                )
                term = o_recv[p, h * 4 + a, 0:R, :].astype(F32) * share[:R]
                mean = term if mean is None else mean + term
            attended[p * R : (p + 1) * R, h * HS : (h + 1) * HS] = mean.astype(BF)

    def rs_copies(p, phase, k):
        upper, lower = halves(R, p)
        if k > 0:
            upper = lower = pl.ds(0, R)
        send, recv, sems = rs_send.at[phase, p], rs_recv.at[phase, p], rs_sem.at[phase, p]
        return (
            remote(send.at[0, k, upper], recv.at[0, k, upper], sems.at[0, k, 0], sems.at[0, k, 1], head=right),
            remote(send.at[1, k, lower], recv.at[1, k, lower], sems.at[1, k, 0], sems.at[1, k, 1], head=left),
        )

    def rs_step(p, phase, block, k):
        upper, lower = halves(R, p)
        send, recv = rs_send.at[phase, p], rs_recv.at[phase, p]
        if k == 0:
            term = block((z + 4) & 7).astype(BF)
            send[0, 0, upper, :] = term[upper.start : upper.start + upper.size]
            send[1, 0, lower, :] = term[lower.start : lower.start + lower.size]
            for copy in rs_copies(p, phase, 0):
                copy.start()
            return
        ahead = block((z + 4 - k) & 7)
        behind = block((z + 4 + k) & 7)
        go, back = rs_copies(p, phase, k - 1)
        go_next, back_next = rs_copies(p, phase, k)
        go.wait_recv()
        if k == 1:
            n = upper.size
            send[0, k, upper, :] = (ahead[:n] + recv[0, 0, upper, :].astype(F32)).astype(BF)
            send[0, k, lower, :] = ahead[n:].astype(BF)
        else:
            send[0, k] = (ahead + recv[0, k - 1].astype(F32)).astype(BF)
        go_next.start()
        back.wait_recv()
        if k == 1:
            send[1, k, upper, :] = behind[:n].astype(BF)
            send[1, k, lower, :] = (behind[n:] + recv[1, 0, lower, :].astype(F32)).astype(BF)
        else:
            send[1, k] = (behind + recv[1, k - 1].astype(F32)).astype(BF)
        back_next.start()

    def rs_end(p, phase, block):
        own = block(z)
        go, back = rs_copies(p, phase, 3)
        go.wait_recv()
        back.wait_recv()
        recv = rs_recv.at[phase, p]
        return own + recv[0, 3].astype(F32) + recv[1, 3].astype(F32)

    def rs_drain(p, phase):
        for k in range(4):
            for copy in rs_copies(p, phase, k):
                copy.wait_send()

    def out_block(p):
        def block(f):
            lanes = pl.ds(pl.multiple_of(f * FB, FB), FB)
            return jnp.dot(
                attended[p * R : (p + 1) * R, :], wout[:, lanes], preferred_element_type=F32
            )

        return block

    def down_block(p):
        def block(f):
            lanes = pl.ds(pl.multiple_of(f * FB, FB), FB)
            return jnp.dot(
                hidden[p * R : (p + 1) * R, :], wdown[:, lanes], preferred_element_type=F32
            )

        return block

    def mix(p):
        rows = pl.ds(p * R, R)
        summed = rs_end(p, 0, out_block(p))
        mixed_all[p, z] = (own_stream[rows, :].astype(F32) + summed).astype(BF)

    def up_part(p, f, own=False):
        rows = pl.ds(p * R, R)
        wide = mixed_all[p, f].astype(F32)
        square = wide * wide
        square = square[:, :128] + square[:, 128:]
        lanes = pl.ds(pl.multiple_of(f * FB, FB), FB)
        normed = (wide * gain2_ref[:, lanes]).astype(BF)
        piece = jnp.dot(normed, wup[lanes, :], preferred_element_type=F32)
        if own:
            acc2[rows, :] = piece
            ssq2[rows, :] = square
        else:
            acc2[rows, :] += piece
            ssq2[rows, :] += square

    def activate(p):
        rows = pl.ds(p * R, R)
        total = jnp.sum(ssq2[rows, :], axis=1, keepdims=True)
        scale = lax.rsqrt(total * (1.0 / D) + 1e-6)
        hidden[rows, :] = jax.nn.gelu(acc2[rows, :] * scale, approximate=True).astype(BF)

    def last(p):
        rows = pl.ds(p * R, R)
        summed = rs_end(p, 1, down_block(p))
        out_ref[rows, :] = (mixed_all[p, z].astype(F32) + summed).astype(BF)

    def embed_work(g, k):
        embed_block(g, (z - 1 - k) & 7)
        if k < 3:
            embed_block(g, (z + 1 + k) & 7)

    def chain(p):
        give_wait(p)
        combine(p)
        for k in range(4):
            rs_step(p, 0, out_block(p), k)
            yield
        mix(p)
        ag_start(*mix_args[p], 0)
        yield
        up_part(p, z, own=True)
        for k in range(4):
            ag_step(*mix_args[p], k)
            if k < 3:
                yield
                up_part(p, (z + 1 + k) & 7)
            up_part(p, (z - 1 - k) & 7)
        activate(p)
        for k in range(4):
            rs_step(p, 1, down_block(p), k)
            yield
        last(p)
        yield

    for k in range(4):
        ag_step(*emb_args, k)
        for p in range(PARTS):
            ag_step(*pos_args[p], k)
            if k == 3:
                embed_work(p, k)
                project(p)
                exchange_start(p)
        if 0 < k < 3:
            for p in range(PARTS):
                embed_work(p, k - 1)
                if k == 2:
                    embed_work(p, k)
        if k == 0:
            wait_cells()
            pool_inputs()
            weights[0].wait()
            for p in range(PARTS):
                embed_block(p, z, own=True)
    queries_start()
    for i in range(1, 4):
        weights[i].wait()
    for p in range(PARTS):
        exchange_wait(p)
    attend()
    chains = [chain(p) for p in range(PARTS)]
    while chains:
        for each in list(chains):
            if next(each, 0) == 0:
                chains.remove(each)

    each_taker(lambda copy: copy.wait_send())
    give_drain()
    ag_drain(*emb_args)
    for g in range(PARTS):
        exchange_drain(g)
    for p in range(PARTS):
        ag_drain(*pos_args[p])
        rs_drain(p, 0)
        ag_drain(*mix_args[p])
        rs_drain(p, 1)


def body(latent, pos, embed, gain1, qkv_w, out_w, gain2, up, down):
    vmem = pl.BlockSpec(memory_space=pltpu.VMEM)
    hbm = pl.BlockSpec(memory_space=pl.ANY)
    dma = pltpu.SemaphoreType.DMA
    return pl.pallas_call(
        kernel,
        out_shape=jax.ShapeDtypeStruct((TOK, FB), BF),
        in_specs=[vmem, hbm, hbm, vmem, hbm, hbm, vmem, hbm, hbm],
        out_specs=vmem,
        scratch_shapes=[
            pltpu.VMEM((3, D, FB), BF),
            pltpu.VMEM((FB, D), BF),
            pltpu.VMEM((D, HID), BF),
            pltpu.VMEM((HID, D), BF),
            pltpu.VMEM((32, 64, 128), BF),
            pltpu.VMEM((NZ, TOK, FB), BF),
            pltpu.VMEM((NZ, C, FB), BF),
            pltpu.VMEM((TOK, 2048), BF),
            pltpu.VMEM((32, 128), F32),
            pltpu.VMEM((3, TOK, C), BF),
            pltpu.VMEM((TOK, FB), BF),
            pltpu.VMEM((TOK, 3 * FB), F32),
            pltpu.VMEM((TOK, 128), F32),
            pltpu.VMEM((2, TOK, 2 * HS), BF),
            pltpu.VMEM((2, TOK, HS), BF),
            pltpu.VMEM((KEYS, 2 * HS), BF),
            pltpu.VMEM((KEYS, HS), BF),
            pltpu.VMEM((PARTS, 8, MSG, HS), BF),
            pltpu.VMEM((PARTS, 8, MSG, HS), BF),
            pltpu.VMEM((2, TOK, 2 * HS), F32),
            pltpu.VMEM((2, TOK, 128), F32),
            pltpu.VMEM((TOK, FB), BF),
            pltpu.VMEM((2, PARTS, 2, 4, R, FB), BF),
            pltpu.VMEM((2, PARTS, 2, 4, R, FB), BF),
            pltpu.VMEM((PARTS, NZ, R, FB), BF),
            pltpu.VMEM((TOK, HID), F32),
            pltpu.VMEM((TOK, 128), F32),
            pltpu.VMEM((TOK, HID), BF),
            dma((6,)),
            dma((6,)),
            dma((32,)),
            dma((PARTS, 2, 4, 2)),
            dma((2, 4, 2)),
            dma((PARTS, 7)),
            dma((PARTS, 8)),
            dma((PARTS, 7)),
            dma((PARTS, 8)),
            dma((PARTS, 8)),
            dma((PARTS, 8)),
            dma((2, PARTS, 2, 4, 2)),
            dma((PARTS, 2, 4, 2)),
        ],
        compiler_params=pltpu.CompilerParams(
            collective_id=0, has_side_effects=True, vmem_limit_bytes=56 * 2**20
        ),
    )(
        latent,
        pos,
        embed,
        gain1.reshape(1, D),
        qkv_w,
        out_w,
        gain2.reshape(1, D),
        up,
        down,
    )


def solution(mesh):
    in_specs = (
        P("seq", None),
        P("seq", "head"),
        P(None, "head"),
        P(),
        P(None, None, "head"),
        P("head", None),
        P(),
        P(None, "head"),
        P("head", None),
    )
    return jax.shard_map(
        body, mesh=mesh, in_specs=in_specs, out_specs=P("seq", "head"), check_vma=False
    )
```

```python
import functools

import jax
import jax.numpy as jnp
from jax import lax
from jax.experimental import pallas as pl
from jax.experimental.pallas import tpu as pltpu
from jax.sharding import PartitionSpec as P

D = 2048
HS = 128
C = 32
TOK = 336
FB = 256
HID = 512
FIRST = 512
SECOND = 2560
PARTS = 3
R = TOK // PARTS
MSG = R + 16
NZ = 8
KEYS = 8 * TOK
NEG = -1e30
QSCALE = 1.4426950408889634 / HS**0.5
MESH = pl.DeviceIdType.MESH
BF = jnp.bfloat16
F32 = jnp.float32
NT = (((1,), (1,)), ((), ()))


def split3(wide):
    high = wide.astype(BF)
    rest = wide - high.astype(F32)
    mid = rest.astype(BF)
    low = (rest - mid.astype(F32)).astype(BF)
    return high, mid, low


def level(token):
    return (token >= FIRST).astype(jnp.int32) + (token >= SECOND).astype(jnp.int32)


def halves(rows, p):
    first = ((rows // 16 + p % 2) // 2) * 16
    return pl.ds(0, first), pl.ds(first, rows - first)


def kernel(
    latent_ref,
    pos_hbm,
    embed_hbm,
    gain1_ref,
    qkv_hbm,
    out_w_hbm,
    gain2_ref,
    up_hbm,
    down_hbm,
    out_ref,
    wqkv,
    wout,
    wup,
    wdown,
    grid_cells,
    pos_all,
    emb_all,
    select,
    lines_buf,
    inp,
    own_stream,
    acc,
    ssq,
    kv_send,
    q_send,
    kv_buf,
    q_buf,
    o_send,
    o_recv,
    state_o,
    state_m,
    attended,
    rs_send,
    rs_recv,
    mixed_all,
    acc2,
    ssq2,
    hidden,
    local_sem,
    cell_ssem,
    cell_rsem,
    pos_sem,
    emb_sem,
    kv_ssem,
    kv_rsem,
    q_ssem,
    q_rsem,
    o_ssem,
    o_rsem,
    rs_sem,
    mix_sem,
):
    seq = lax.axis_index("seq")
    z = lax.axis_index("head")
    x, y, c = seq >> 3, (seq >> 1) & 3, seq & 1
    right, left = (z + 1) & 7, (z + 7) & 7
    a0 = jnp.where(c == 0, x, y)
    b0 = jnp.where(c == 0, y, x)

    def sid(px, py, pc):
        return (px * 4 + py) * 2 + pc

    def ring(value, step):
        return (value + step) & 3

    sibling = sid(x, y, 1 - c)

    loads = [
        pltpu.make_async_copy(pos_hbm, pos_all.at[z], local_sem.at[0])
    ]
    loads.append(pltpu.make_async_copy(embed_hbm, emb_all.at[z], local_sem.at[1]))
    weights = [
        pltpu.make_async_copy(src, dst, local_sem.at[2 + i])
        for i, (src, dst) in enumerate(
            ((qkv_hbm, wqkv), (out_w_hbm, wout), (up_hbm, wup), (down_hbm, wdown))
        )
    ]
    for load in loads:
        load.start()
    for load in weights:
        load.start()

    wide = latent_ref[...].astype(F32)
    both = wide[0:1] + wide[1:2]
    for j in range(32):
        lines_buf[j : j + 1, :] = both[:, j * 128 : (j + 1) * 128]
    wide = lines_buf[...] * 0.25
    pooled = jnp.concatenate(
        [wide[:, 0:C] + wide[:, C : 2 * C], wide[:, 2 * C : 3 * C] + wide[:, 3 * C :]], axis=0
    )
    grid_cells[...] = jnp.zeros((32, 64, 128), BF)
    grid_cells[seq] = jnp.concatenate([*split3(pooled), jnp.zeros((64, C), BF)], axis=1)

    token = seq * TOK + lax.broadcasted_iota(jnp.int32, (TOK, 1), 0)
    top, mid_level = token >= SECOND, token >= FIRST
    from_top, from_mid = token - SECOND, token - FIRST
    key_top = (from_top >> 8) * 64 + ((from_top & 127) >> 1)
    key_mid = (from_mid >> 7) * 32 + ((from_mid & 63) >> 1)
    fine_key = jnp.where(top, key_top, -1)
    coarse_key = jnp.where(top, -1, jnp.where(mid_level, key_mid, token))
    col = lax.broadcasted_iota(jnp.int32, (1, 2048), 1)
    cell_row, cell_col = col >> 6, (col & 31) * 2 + ((col >> 5) & 1)
    fine_col = cell_row * 64 + cell_col
    coarse_col = (cell_row >> 1) * 32 + (cell_col >> 1)
    select[...] = jnp.where(
        fine_key == fine_col, 1.0, jnp.where(coarse_key == coarse_col, 0.25, 0.0)
    ).astype(BF)

    barrier = pltpu.get_barrier_semaphore()
    pl.semaphore_signal(barrier, inc=1, device_id={"head": right}, device_id_type=MESH)
    pl.semaphore_signal(barrier, inc=1, device_id={"head": left}, device_id_type=MESH)
    for step in range(1, 32):
        peer = (seq + step) & 31
        pl.semaphore_signal(barrier, inc=1, device_id={"seq": peer}, device_id_type=MESH)
    pl.semaphore_wait(barrier, 33)

    def remote(src, dst, ssem, rsem, **where):
        return pltpu.make_async_remote_copy(
            src_ref=src,
            dst_ref=dst,
            send_sem=ssem,
            recv_sem=rsem,
            device_id=where,
            device_id_type=MESH,
        )

    def ag_copies(buf, sems, base, rows, p, k):
        go, back = (z - k) & 7, (z + k) & 7
        if k == 3:
            upper, lower = halves(rows, p)
            upper = pl.ds(base + upper.start, upper.size)
            lower = pl.ds(base + lower.start, lower.size)
        else:
            upper = lower = pl.ds(base, rows)
        return (
            remote(buf.at[go, upper], buf.at[go, upper], sems.at[0, k, 0], sems.at[0, k, 1], head=right),
            remote(buf.at[back, lower], buf.at[back, lower], sems.at[1, k, 0], sems.at[1, k, 1], head=left),
        )

    def ag_start(*args):
        for copy in ag_copies(*args):
            copy.start()

    def ag_step(*args):
        *where, k = args
        here = ag_copies(*where, k)
        if k == 3:
            for copy in here:
                copy.wait_recv()
            return
        for copy, onward in zip(here, ag_copies(*where, k + 1)):
            copy.wait_recv()
            onward.start()

    def ag_drain(*args):
        for k in range(4):
            for copy in ag_copies(*args, k):
                copy.wait_send()

    pos_args = [(pos_all, pos_sem.at[p], p * R, R, p) for p in range(PARTS)]
    emb_args = (emb_all, emb_sem, 0, C, 0)
    mix_args = [(mixed_all.at[p], mix_sem.at[p], 0, R, p) for p in range(PARTS)]

    for load in loads:
        load.wait()
    ag_start(*emb_args, 0)
    for p in range(PARTS):
        ag_start(*pos_args[p], 0)

    def takers(row):
        fine, coarse = SECOND + 256 * row, row >> 1
        middle, low = FIRST + 128 * coarse, 32 * coarse
        return (fine, fine + 255), (middle, middle + 127), (low, low + 31)

    def owner(token):
        return (token * 49933) >> 24

    def cell_copy(i, row, dest):
        return remote(
            grid_cells.at[row], grid_cells.at[row], cell_ssem.at[i], cell_rsem.at[row], seq=dest
        )

    def each_taker(act):
        for i, ends in enumerate(takers(seq)):
            one, two = owner(ends[0]), owner(ends[1])

            @pl.when(one != seq)
            def _():
                act(cell_copy(2 * i, seq, one))

            @pl.when(jnp.logical_and(two != one, two != seq))
            def _():
                act(cell_copy(2 * i + 1, seq, two))

    each_taker(lambda copy: copy.start())

    def wait_cells():
        start, end = seq * TOK, seq * TOK + TOK - 1

        def wait_rows(low, high):
            @pl.loop(low, high)
            def _(row):
                @pl.when(row != seq)
                def _():
                    cell_copy(0, row, sibling).wait_recv()

        @pl.when(end >= SECOND)
        def _():
            wait_rows(jnp.maximum(start - SECOND, 0) >> 8, ((end - SECOND) >> 8) + 1)

        @pl.when(jnp.logical_and(end >= FIRST, start < SECOND))
        def _():
            wait_rows(
                (jnp.maximum(start - FIRST, 0) >> 7) * 2,
                ((jnp.minimum(end, SECOND - 1) - FIRST) >> 7) * 2 + 2,
            )

        @pl.when(start < FIRST)
        def _():
            wait_rows((start >> 5) * 2, (jnp.minimum(end, FIRST - 1) >> 5) * 2 + 2)

    def pool_inputs():
        pooled = jnp.dot(
            select[...], grid_cells[...].reshape(2048, 128), preferred_element_type=F32
        )
        inputs = pooled[:, 0:C] + pooled[:, C : 2 * C] + pooled[:, 2 * C : 3 * C]
        for i, piece in enumerate(split3(inputs)):
            inp[i] = piece

    def group_rows(p):
        return pl.ds(p * R, R)

    def embed_block(g, f, own=False):
        rows = group_rows(g)
        emb = emb_all[f]
        wide = pos_all[f, rows, :].astype(F32)
        for i in range(3):
            wide = wide + jnp.dot(inp[i, rows, :], emb, preferred_element_type=F32)
        stream = wide.astype(BF)
        if own:
            own_stream[rows, :] = stream
        wide = stream.astype(F32)
        square = wide * wide
        square = square[:, :128] + square[:, 128:]
        lanes = pl.ds(pl.multiple_of(f * FB, FB), FB)
        normed = (wide * gain1_ref[:, lanes]).astype(BF)
        for j in range(3):
            piece = jnp.dot(normed, wqkv[j, lanes, :], preferred_element_type=F32)
            if own:
                acc[rows, j * FB : (j + 1) * FB] = piece
            else:
                acc[rows, j * FB : (j + 1) * FB] += piece
        if own:
            ssq[rows, :] = square
        else:
            ssq[rows, :] += square

    def project(g):
        rows = group_rows(g)
        total = jnp.sum(ssq[rows, :], axis=1, keepdims=True)
        scale = lax.rsqrt(total * (1.0 / D) + 1e-6)
        for h in range(2):
            cols = slice(h * HS, (h + 1) * HS)
            q_send[h, rows, :] = (acc[rows, cols] * (scale * QSCALE)).astype(BF)
            kv_send[h, rows, 0:HS] = (acc[rows, FB + h * HS : FB + (h + 1) * HS] * scale).astype(BF)
            kv_send[h, rows, HS:] = (
                acc[rows, 2 * FB + h * HS : 2 * FB + (h + 1) * HS] * scale
            ).astype(BF)

    def slot_rows(slot, g):
        return pl.ds(pl.multiple_of(slot * TOK + g * R, 16), R)

    def exchange(p):
        rows = group_rows(p)
        kv_copies, q_copies = [], []

        def kv_copy(i, head, slot, dest):
            return remote(
                kv_send.at[head, rows],
                kv_buf.at[slot_rows(slot, p)],
                kv_ssem.at[p, i],
                kv_rsem.at[p, slot],
                seq=dest,
            )

        def q_copy(i, head, slot, dest):
            return remote(
                q_send.at[head, rows],
                q_buf.at[slot_rows(slot, p)],
                q_ssem.at[p, i],
                q_rsem.at[p, slot],
                seq=dest,
            )

        other = 1 - c
        kv_copies.append(kv_copy(6, other, jnp.where(c == 1, x, y) * 2 + c, sibling))
        q_copies.append(q_copy(6, other, jnp.where(c == 1, y, x) * 2 + c, sibling))
        for i, step in enumerate((3, 2, 1)):
            kv_copies.append(kv_copy(i, 0, x * 2 + c, sid(ring(x, step), y, 0)))
            kv_copies.append(kv_copy(3 + i, 1, y * 2 + c, sid(x, ring(y, step), 1)))
            q_copies.append(q_copy(i, 0, y * 2 + c, sid(x, ring(y, step), 0)))
            q_copies.append(q_copy(3 + i, 1, x * 2 + c, sid(ring(x, step), y, 1)))
        return kv_copies, q_copies

    def exchange_start(p):
        rows = group_rows(p)
        for copy in exchange(p)[0]:
            copy.start()
        kv_buf[slot_rows(a0 * 2 + c, p), :] = kv_send[c, rows, :]
        q_buf[slot_rows(b0 * 2 + c, p), :] = q_send[c, rows, :]

    def queries_start():
        copies = [exchange(p)[1] for p in range(PARTS)]
        for i in (1, 2, 3, 4, 5, 6, 0):
            for p in range(PARTS):
                copies[p][i].start()

    def queries_wait(b):
        @pl.loop(0, 2)
        def _(core):
            slot = b * 2 + core

            @pl.when(slot != b0 * 2 + c)
            def _():
                for p in range(PARTS):
                    remote(
                        q_send.at[0, group_rows(p)],
                        q_buf.at[slot_rows(slot, p)],
                        q_ssem.at[p, 0],
                        q_rsem.at[p, slot],
                        seq=sibling,
                    ).wait_recv()

    def exchange_wait(p):
        rows = group_rows(p)
        for i in range(1, 8):
            slot = (a0 * 2 + c + i) & 7
            remote(
                kv_send.at[0, rows],
                kv_buf.at[slot_rows(slot, p)],
                kv_ssem.at[p, 0],
                kv_rsem.at[p, slot],
                seq=sibling,
            ).wait_recv()

    def exchange_drain(p):
        kv_copies, q_copies = exchange(p)
        for copy in q_copies + kv_copies:
            copy.wait_send()

    ones_row = jnp.ones((1, HS), BF)

    def values_and_ones(kv):
        return jnp.concatenate([kv[:, HS:], jnp.broadcast_to(ones_row, (kv.shape[0], HS))], axis=1)

    diag = lax.broadcasted_iota(jnp.int32, (128, 128), 0) == lax.broadcasted_iota(
        jnp.int32, (128, 128), 1
    )

    def finish(slot, total, largest):
        sums = total[:, HS:]
        normal = (total[:, :HS] / sums).astype(BF)
        log_sum = largest + jnp.log2(sums)
        for p in range(PARTS):
            low = p * R
            o_send[p, slot, 0:R, :] = normal[low : low + R]
            tile = jnp.concatenate(
                [log_sum[low : low + R], jnp.zeros((128 - R, 128), F32)], axis=0
            )
            line = jnp.sum(jnp.where(diag, tile, 0.0), axis=0, keepdims=True)
            packed = [v.astype(F32) for v in split3(line)] + [jnp.zeros((13, 128), F32)]
            o_send[p, slot, R:MSG, :] = jnp.concatenate(packed, axis=0).astype(BF)

    CHUNK = 896

    def plain_slot(slot):
        queries = q_buf[pl.ds(pl.multiple_of(slot * TOK, 16), TOK), :]
        largest = total = None
        for low in range(0, KEYS, CHUNK):
            kv = kv_buf[low : low + CHUNK, :]
            scores = lax.dot_general(queries, kv[:, :HS], NT, preferred_element_type=F32)
            newest = jnp.max(scores, axis=1, keepdims=True)
            if total is not None:
                newest = jnp.maximum(newest, largest)
            weights = jnp.exp2(scores - newest).astype(BF)
            part = jnp.dot(weights, values_and_ones(kv), preferred_element_type=F32)
            total = part if total is None else total * jnp.exp2(largest - newest) + part
            largest = newest
        finish(slot, total, largest)

    def masked_block(b, chunks):
        first_q = jnp.where(c == 0, x * 8 + b * 2, b * 8 + y * 2)
        state_m[...] = jnp.full((2, TOK, 128), NEG, F32)
        state_o[...] = jnp.zeros((2, TOK, 2 * HS), F32)

        @pl.loop(0, chunks)
        def _(i):
            low = pl.multiple_of(i * CHUNK, 128)
            kv = kv_buf[pl.ds(low, CHUNK), :]
            key = low + lax.broadcasted_iota(jnp.int32, (1, CHUNK), 1)
            block = sum((key >= edge * 2 * TOK).astype(jnp.int32) for edge in (1, 2, 3))
            shift = jnp.where(c == 0, block * (6 * TOK) + y * 2 * TOK, x * 8 * TOK)
            k_level = level(key + shift)
            for core in range(2):
                row = pl.multiple_of((b * 2 + core) * TOK, 16)
                queries = q_buf[pl.ds(row, TOK), :]
                scores = lax.dot_general(queries, kv[:, :HS], NT, preferred_element_type=F32)
                token = (first_q + core) * TOK + lax.broadcasted_iota(jnp.int32, (TOK, 1), 0)
                scores = jnp.where(k_level <= level(token), scores, NEG)
                before = state_m[core, :, 0:1]
                newest = jnp.maximum(before, jnp.max(scores, axis=1, keepdims=True))
                weights = jnp.exp2(scores - newest).astype(BF)
                part = jnp.dot(weights, values_and_ones(kv), preferred_element_type=F32)
                state_o[core] = state_o[core] * jnp.exp2(before - newest) + part
                state_m[core] = jnp.broadcast_to(newest, (TOK, 128))

        @pl.loop(0, 2)
        def _(core):
            finish(b * 2 + core, state_o[core], state_m[core, :, 0:1])

    def give_copies(slot, act, keep):
        b, core = slot >> 1, slot & 1
        dest = jnp.where(c == 0, sid(x, b, core), sid(b, y, core))

        @pl.when(dest != seq)
        def _():
            for p in range(PARTS):
                act(
                    remote(
                        o_send.at[p, slot],
                        o_recv.at[p, c * 4 + b0],
                        o_ssem.at[p, slot],
                        o_rsem.at[p, c * 4 + b0],
                        seq=dest,
                    )
                )

        if keep:

            @pl.when(dest == seq)
            def _():
                for p in range(PARTS):
                    o_recv[p, c * 4 + b0] = o_send[p, slot]

    def give_block(b):
        @pl.loop(0, 2)
        def _(core):
            give_copies(b * 2 + core, lambda copy: copy.start(), True)

    def give_drain():
        @pl.loop(0, 8)
        def _(slot):
            give_copies(slot, lambda copy: copy.wait_send(), False)

    def attend():
        first_plain = jnp.where(c == 0, jnp.where(x == 0, 4, 0), 1)
        nothing = jnp.logical_and(c == 1, jnp.logical_and(x >= 1, y < 3))

        @pl.when(nothing)
        def _():
            for i in range(2):
                for p in range(PARTS):
                    o_send[p, i, 0:R, :] = jnp.zeros((R, HS), BF)
                    o_send[p, i, R:MSG, :] = jnp.full((MSG - R, HS), NEG, BF)
            give_block(0)

        @pl.when(jnp.logical_not(nothing))
        def _():
            @pl.loop(0, first_plain)
            def _(b):
                queries_wait(b)
                masked_block(b, jnp.where(jnp.logical_and(c == 0, b < 3), 1, 3))
                give_block(b)

        @pl.loop(first_plain, 4)
        def _(i):
            turn = b0 + i - first_plain
            turn = jnp.where(turn >= 3, turn - 3, turn)
            b = jnp.where(c == 0, (b0 + 1 + i) & 3, 1 + turn)
            queries_wait(b)
            plain_slot(b * 2)
            plain_slot(b * 2 + 1)
            give_block(b)

        @pl.when(nothing)
        def _():
            queries_wait(0)

    def give_wait(p):
        for i in range(1, 8):
            slot = (c * 4 + b0 + i) & 7
            remote(
                o_send.at[p, 0],
                o_recv.at[p, slot],
                o_ssem.at[p, 0],
                o_rsem.at[p, slot],
                seq=sibling,
            ).wait_recv()

    def combine(p):
        tails = [o_recv[p, i, R:MSG, :].astype(F32) for i in range(8)]
        logs = [t[0:1] + t[1:2] + t[2:3] for t in tails]
        for h in range(2):
            four = logs[h * 4 : h * 4 + 4]
            largest = functools.reduce(jnp.maximum, four)
            powers = [jnp.exp2(v - largest) for v in four]
            total = powers[0] + powers[1] + powers[2] + powers[3]
            mean = None
            for a in range(4):
                share = jnp.sum(
                    jnp.where(diag, powers[a] / total, 0.0), axis=1, keepdims=True
                )
                term = o_recv[p, h * 4 + a, 0:R, :].astype(F32) * share[:R]
                mean = term if mean is None else mean + term
            attended[p * R : (p + 1) * R, h * HS : (h + 1) * HS] = mean.astype(BF)

    def rs_copies(p, phase, k):
        upper, lower = halves(R, p)
        if k > 0:
            upper = lower = pl.ds(0, R)
        send, recv, sems = rs_send.at[phase, p], rs_recv.at[phase, p], rs_sem.at[phase, p]
        return (
            remote(send.at[0, k, upper], recv.at[0, k, upper], sems.at[0, k, 0], sems.at[0, k, 1], head=right),
            remote(send.at[1, k, lower], recv.at[1, k, lower], sems.at[1, k, 0], sems.at[1, k, 1], head=left),
        )

    def rs_step(p, phase, block, k):
        upper, lower = halves(R, p)
        send, recv = rs_send.at[phase, p], rs_recv.at[phase, p]
        if k == 0:
            term = block((z + 4) & 7).astype(BF)
            send[0, 0, upper, :] = term[upper.start : upper.start + upper.size]
            send[1, 0, lower, :] = term[lower.start : lower.start + lower.size]
            for copy in rs_copies(p, phase, 0):
                copy.start()
            return
        ahead = block((z + 4 - k) & 7)
        behind = block((z + 4 + k) & 7)
        go, back = rs_copies(p, phase, k - 1)
        go_next, back_next = rs_copies(p, phase, k)
        go.wait_recv()
        if k == 1:
            n = upper.size
            send[0, k, upper, :] = (ahead[:n] + recv[0, 0, upper, :].astype(F32)).astype(BF)
            send[0, k, lower, :] = ahead[n:].astype(BF)
        else:
            send[0, k] = (ahead + recv[0, k - 1].astype(F32)).astype(BF)
        go_next.start()
        back.wait_recv()
        if k == 1:
            send[1, k, upper, :] = behind[:n].astype(BF)
            send[1, k, lower, :] = (behind[n:] + recv[1, 0, lower, :].astype(F32)).astype(BF)
        else:
            send[1, k] = (behind + recv[1, k - 1].astype(F32)).astype(BF)
        back_next.start()

    def rs_end(p, phase, block):
        own = block(z)
        go, back = rs_copies(p, phase, 3)
        go.wait_recv()
        back.wait_recv()
        recv = rs_recv.at[phase, p]
        return own + recv[0, 3].astype(F32) + recv[1, 3].astype(F32)

    def rs_drain(p, phase):
        for k in range(4):
            for copy in rs_copies(p, phase, k):
                copy.wait_send()

    def out_block(p):
        def block(f):
            lanes = pl.ds(pl.multiple_of(f * FB, FB), FB)
            return jnp.dot(
                attended[p * R : (p + 1) * R, :], wout[:, lanes], preferred_element_type=F32
            )

        return block

    def down_block(p):
        def block(f):
            lanes = pl.ds(pl.multiple_of(f * FB, FB), FB)
            return jnp.dot(
                hidden[p * R : (p + 1) * R, :], wdown[:, lanes], preferred_element_type=F32
            )

        return block

    def mix(p):
        rows = pl.ds(p * R, R)
        summed = rs_end(p, 0, out_block(p))
        mixed_all[p, z] = (own_stream[rows, :].astype(F32) + summed).astype(BF)

    def up_part(p, f, own=False):
        rows = pl.ds(p * R, R)
        wide = mixed_all[p, f].astype(F32)
        square = wide * wide
        square = square[:, :128] + square[:, 128:]
        lanes = pl.ds(pl.multiple_of(f * FB, FB), FB)
        normed = (wide * gain2_ref[:, lanes]).astype(BF)
        piece = jnp.dot(normed, wup[lanes, :], preferred_element_type=F32)
        if own:
            acc2[rows, :] = piece
            ssq2[rows, :] = square
        else:
            acc2[rows, :] += piece
            ssq2[rows, :] += square

    def activate(p):
        rows = pl.ds(p * R, R)
        total = jnp.sum(ssq2[rows, :], axis=1, keepdims=True)
        scale = lax.rsqrt(total * (1.0 / D) + 1e-6)
        hidden[rows, :] = jax.nn.gelu(acc2[rows, :] * scale, approximate=True).astype(BF)

    def last(p):
        rows = pl.ds(p * R, R)
        summed = rs_end(p, 1, down_block(p))
        out_ref[rows, :] = (mixed_all[p, z].astype(F32) + summed).astype(BF)

    def embed_work(g, k):
        embed_block(g, (z - 1 - k) & 7)
        if k < 3:
            embed_block(g, (z + 1 + k) & 7)

    def chain(p):
        give_wait(p)
        combine(p)
        for k in range(4):
            rs_step(p, 0, out_block(p), k)
            yield
        mix(p)
        ag_start(*mix_args[p], 0)
        yield
        up_part(p, z, own=True)
        for k in range(4):
            ag_step(*mix_args[p], k)
            if k < 3:
                yield
                up_part(p, (z + 1 + k) & 7)
            up_part(p, (z - 1 - k) & 7)
        activate(p)
        for k in range(4):
            rs_step(p, 1, down_block(p), k)
            yield
        last(p)
        yield

    for k in range(4):
        ag_step(*emb_args, k)
        for p in range(PARTS):
            ag_step(*pos_args[p], k)
            if k == 3:
                embed_work(p, k)
                project(p)
                exchange_start(p)
        if 0 < k < 3:
            for p in range(PARTS):
                embed_work(p, k - 1)
                if k == 2:
                    embed_work(p, k)
        if k == 0:
            wait_cells()
            pool_inputs()
            weights[0].wait()
            for p in range(PARTS):
                embed_block(p, z, own=True)
    queries_start()
    for i in range(1, 4):
        weights[i].wait()
    for p in range(PARTS):
        exchange_wait(p)
    attend()
    late = [lambda: (each_taker(lambda copy: copy.wait_send()), ag_drain(*emb_args))]
    late += [functools.partial(ag_drain, *pos_args[p]) for p in range(PARTS)]
    late += [functools.partial(exchange_drain, p) for p in range(PARTS)]
    late += [give_drain]
    late += [lambda: [rs_drain(p, 0) for p in range(PARTS)]]
    late += [lambda: None]
    late += [lambda: [ag_drain(*mix_args[p]) for p in range(PARTS)]]
    chains = [chain(p) for p in range(PARTS)]
    while chains:
        for each in list(chains):
            if next(each, 0) == 0:
                chains.remove(each)
        if late:
            late.pop(0)()

    for p in range(PARTS):
        rs_drain(p, 1)


def body(latent, pos, embed, gain1, qkv_w, out_w, gain2, up, down):
    vmem = pl.BlockSpec(memory_space=pltpu.VMEM)
    hbm = pl.BlockSpec(memory_space=pl.ANY)
    dma = pltpu.SemaphoreType.DMA
    return pl.pallas_call(
        kernel,
        out_shape=jax.ShapeDtypeStruct((TOK, FB), BF),
        in_specs=[vmem, hbm, hbm, vmem, hbm, hbm, vmem, hbm, hbm],
        out_specs=vmem,
        scratch_shapes=[
            pltpu.VMEM((3, D, FB), BF),
            pltpu.VMEM((FB, D), BF),
            pltpu.VMEM((D, HID), BF),
            pltpu.VMEM((HID, D), BF),
            pltpu.VMEM((32, 64, 128), BF),
            pltpu.VMEM((NZ, TOK, FB), BF),
            pltpu.VMEM((NZ, C, FB), BF),
            pltpu.VMEM((TOK, 2048), BF),
            pltpu.VMEM((32, 128), F32),
            pltpu.VMEM((3, TOK, C), BF),
            pltpu.VMEM((TOK, FB), BF),
            pltpu.VMEM((TOK, 3 * FB), F32),
            pltpu.VMEM((TOK, 128), F32),
            pltpu.VMEM((2, TOK, 2 * HS), BF),
            pltpu.VMEM((2, TOK, HS), BF),
            pltpu.VMEM((KEYS, 2 * HS), BF),
            pltpu.VMEM((KEYS, HS), BF),
            pltpu.VMEM((PARTS, 8, MSG, HS), BF),
            pltpu.VMEM((PARTS, 8, MSG, HS), BF),
            pltpu.VMEM((2, TOK, 2 * HS), F32),
            pltpu.VMEM((2, TOK, 128), F32),
            pltpu.VMEM((TOK, FB), BF),
            pltpu.VMEM((2, PARTS, 2, 4, R, FB), BF),
            pltpu.VMEM((2, PARTS, 2, 4, R, FB), BF),
            pltpu.VMEM((PARTS, NZ, R, FB), BF),
            pltpu.VMEM((TOK, HID), F32),
            pltpu.VMEM((TOK, 128), F32),
            pltpu.VMEM((TOK, HID), BF),
            dma((6,)),
            dma((6,)),
            dma((32,)),
            dma((PARTS, 2, 4, 2)),
            dma((2, 4, 2)),
            dma((PARTS, 7)),
            dma((PARTS, 8)),
            dma((PARTS, 7)),
            dma((PARTS, 8)),
            dma((PARTS, 8)),
            dma((PARTS, 8)),
            dma((2, PARTS, 2, 4, 2)),
            dma((PARTS, 2, 4, 2)),
        ],
        compiler_params=pltpu.CompilerParams(
            collective_id=0, has_side_effects=True, vmem_limit_bytes=56 * 2**20
        ),
    )(
        latent,
        pos,
        embed,
        gain1.reshape(1, D),
        qkv_w,
        out_w,
        gain2.reshape(1, D),
        up,
        down,
    )


def solution(mesh):
    in_specs = (
        P("seq", None),
        P("seq", "head"),
        P(None, "head"),
        P(),
        P(None, None, "head"),
        P("head", None),
        P(),
        P(None, "head"),
        P("head", None),
    )
    return jax.shard_map(
        body, mesh=mesh, in_specs=in_specs, out_specs=P("seq", "head"), check_vma=False
    )
```
